128 devices in a mesh: section: 8 (over x, core), ctx: 16 (over z, y).
Axes of the slice: x: 4, y: 4, z: 4, core: 2. Of those that a mesh axis runs over, the one named last changes fastest.
Arguments:
- segment_input: bfloat16 [8, 2048, 8192], P('section', 'ctx'), may hold values from -6 to 6
- queries: bfloat16 [8, 2048, 8192], P('section', 'ctx'), may hold values from -6 to 6
- keys: bfloat16 [8, 2048, 1024], P('section', 'ctx'), may hold values from -6 to 6
- values: bfloat16 [8, 2048, 1024], P('section', 'ctx'), may hold values from -6 to 6
- cotangent: bfloat16 [8, 2048, 8192], P('section', 'ctx'), may hold values from -6 to 6
- selected: int32 [8, 2048], P('section', 'ctx'), may hold values from 0 to 127, as said below
- counts: int32 [8, 16], P('section', 'ctx'), may hold values from 1 to 128, as said below
Outputs:
- next_input: bfloat16 [8, 2048, 8192], P('section', 'ctx')
- query_grad: bfloat16 [8, 2048, 8192], P('section', 'ctx')
- key_grad: bfloat16 [8, 2048, 1024], P('section', 'ctx')
- value_grad: bfloat16 [8, 2048, 1024], P('section', 'ctx')
The draws below stay inside these ranges and needn't reach their ends.
Inputs may be any that keep to these rules, and one draw needn't show every extreme that they name: Layers of odd index are dense: every count is 128. Layers of even index are routed: counts are at most 32. Each block of 128 entries is a permutation of the block-local indices; its first count entries are the selected ones, in increasing order.
All inputs are finite; a program needn't handle non-finite values.
Results may differ from the reference program's by a relative error of at most 0.019.
Values may be sent and summed in bfloat16 or wider, within the bound.
No kernel may reach another device: no remote copies, remote signals or barrier semaphores. Data moves between devices by JAX's collectives and lax.ppermute only.
A program may use at most 128 MiB of HBM per device.

```python
import jax
import jax.numpy as jnp
from jax import lax

D = 8192
KV_HEADS = 8
HEAD_DIM = 128
ROWS = 128
SEQ = 2048
SECTIONS = 8


def route_counts(key):
    blocks = SEQ // ROWS
    section_ids = jnp.arange(SECTIONS)
    routed = jax.random.randint(key, (SECTIONS, blocks), 1, ROWS // 4 + 1)
    return jnp.where((section_ids % 2 == 1)[:, None], ROWS, routed).astype(jnp.int32)


def route_order(key):
    chosen_counts = route_counts(key)
    shuffle_key = jax.random.fold_in(key, 7)
    blocks = SEQ // ROWS
    shuffled = jax.vmap(lambda single: jax.random.permutation(single, ROWS))(jax.random.split(shuffle_key, SECTIONS * blocks)).reshape(SECTIONS, blocks, ROWS)
    places = jnp.arange(ROWS, dtype=jnp.int32)
    chosen = shuffled < chosen_counts[:, :, None]
    ordered = jnp.argsort(jnp.where(chosen, places, ROWS + places), axis=-1)
    return ordered.astype(jnp.int32).reshape(SECTIONS, SEQ)


def draw_counts(key, part):
    return route_counts(key)


def draw_selected(key, part):
    return route_order(key)


def draw_queries(key, part):
    own_key = jax.random.fold_in(key, 21)
    return jnp.clip(jax.random.normal(own_key, (SECTIONS, SEQ, D), jnp.float32), -6.0, 6.0).astype(jnp.bfloat16)


def draw_keys(key, part):
    own_key = jax.random.fold_in(key, 23)
    return jnp.clip(jax.random.normal(own_key, (SECTIONS, SEQ, KV_HEADS * HEAD_DIM), jnp.float32), -6.0, 6.0).astype(jnp.bfloat16)


def level_of(stream_key, dims, shards, smallest, largest):
    loudness = 1.0
    for axis_at, shards_of in shards:
        draws = jax.random.uniform(jax.random.fold_in(jax.random.fold_in(stream_key, 6), axis_at), (shards_of,), jnp.float32, smallest / len(shards), largest / len(shards))
        loudness = loudness * jnp.repeat(jnp.exp(draws), dims[axis_at] // shards_of).reshape((-1,) + (1,) * (len(dims) - 1 - axis_at))
    return loudness


def noise(key, shape, deviation, reach, cuts=(), kind=jnp.bfloat16):
    entries = deviation * jax.random.normal(key, shape, jnp.float32)
    if cuts:
        entries = entries * level_of(key, shape, cuts, -0.22, 0.18)
    return jnp.clip(entries, -reach, reach).astype(kind)


def setup_inputs(seed: int = 0) -> dict:
    key_list = jax.random.split(jax.random.key(seed), 8)
    segment_input = noise(key_list[0], (SECTIONS, SEQ, D), 1.0, 6.0, ((0, 8), (1, 16)))
    queries = draw_queries(jax.random.fold_in(key_list[7], 71), 0)
    keys = draw_keys(jax.random.fold_in(key_list[7], 71), 0)
    values = noise(key_list[3], (SECTIONS, SEQ, KV_HEADS * HEAD_DIM), 1.0, 6.0, ((0, 8), (1, 16)))
    cotangent = noise(key_list[4], (SECTIONS, SEQ, D), 1.0, 6.0, ((0, 8), (1, 16)))
    selected = draw_selected(jax.random.fold_in(key_list[7], 71), 0)
    counts = draw_counts(jax.random.fold_in(key_list[7], 71), 0)
    return dict(segment_input=segment_input, queries=queries, keys=keys, values=values, cotangent=cotangent, selected=selected, counts=counts)


masked_value = -1e9


def narrow(matrix):
    return lax.optimization_barrier(matrix.astype(jnp.bfloat16)).astype(jnp.float32)


def masked_scores(query_group, key_group, query_place, key_place):
    scaling = query_group.shape[-1] ** -0.5
    allowed = (key_place[None, :] <= query_place[:, None]) & (key_place[None, :] >= 0)
    scores = jnp.einsum("qih,kh->qik", query_group, key_group, preferred_element_type=jnp.float32) * scaling
    return jnp.where(allowed[:, None, :], scores, masked_value)


def attend_group(query_group, key_group, value_group, query_place, key_place):
    scores = masked_scores(query_group, key_group, query_place, key_place)
    maxima = jnp.max(scores, axis=-1, keepdims=True)
    weights = jnp.exp(scores - maxima)
    totals = jnp.sum(weights, axis=-1, keepdims=True)
    prob_b = narrow(weights / totals)
    output = jnp.einsum("qik,kh->qih", prob_b, value_group, preferred_element_type=jnp.float32)
    return output, maxima[..., 0], totals[..., 0]


def both_grads(query_group, key_group, value_group, query_place, key_place, output_group, maxima, totals, out_grad):
    scaling = query_group.shape[-1] ** -0.5
    scores = masked_scores(query_group, key_group, query_place, key_place)
    weights = jnp.exp(scores - maxima[..., None]) / totals[..., None]
    prob_b = narrow(weights)
    along = jnp.einsum("qih,kh->qik", out_grad, value_group, preferred_element_type=jnp.float32)
    deltas = jnp.sum(out_grad * output_group, axis=-1)
    score_grad = narrow(weights * (along - deltas[..., None]))
    query_grad = jnp.einsum("qik,kh->qih", score_grad, key_group, preferred_element_type=jnp.float32) * scaling
    key_grad = jnp.einsum("qik,qih->kh", score_grad, query_group, preferred_element_type=jnp.float32) * scaling
    value_grad = jnp.einsum("qik,qih->kh", prob_b, out_grad, preferred_element_type=jnp.float32)
    return query_grad, key_grad, value_grad


def head_groups(matrix):
    return matrix.reshape(matrix.shape[0], KV_HEADS, -1, HEAD_DIM).transpose(1, 0, 2, 3)


def pair_groups(key_value):
    count_rows = key_value.shape[0]
    width = KV_HEADS * HEAD_DIM
    key_group = key_value[:, :width].reshape(count_rows, KV_HEADS, HEAD_DIM).transpose(1, 0, 2)
    value_group = key_value[:, width:].reshape(count_rows, KV_HEADS, HEAD_DIM).transpose(1, 0, 2)
    return key_group, value_group


def merge_heads(stacked):
    return stacked.transpose(1, 0, 2, 3).reshape(stacked.shape[1], -1)


def merge_groups(stacked):
    return stacked.transpose(1, 0, 2).reshape(stacked.shape[1], -1)


def forward(query_sel, key_value, query_place, key_place):
    key_group, value_group = pair_groups(key_value)
    output, maxima, totals = lax.map(lambda items: attend_group(items[0], items[1], items[2], query_place, key_place), (head_groups(query_sel), key_group, value_group))
    return merge_heads(output), maxima, totals


def backward(query_sel, key_value, query_place, key_place, output, maxima, totals, out_grad):
    key_group, value_group = pair_groups(key_value)
    query_grad, key_grad, value_grad = lax.map(lambda items: both_grads(items[0], items[1], items[2], query_place, key_place, items[3], items[4], items[5], items[6]), (head_groups(query_sel), key_group, value_group, head_groups(output), maxima, totals, head_groups(out_grad)))
    return merge_heads(query_grad), jnp.concatenate([merge_groups(key_grad), merge_groups(value_grad)], 1)


def one_segment(layer_input, layer_queries, layer_keys, layer_values, layer_cotangent, layer_selected, layer_counts):
    blocks = SEQ // ROWS
    slot_ids = jnp.arange(ROWS, dtype=jnp.int32)
    block_sel = layer_selected.reshape(blocks, ROWS)
    is_valid = slot_ids[None, :] < layer_counts[:, None]
    chooser = ((block_sel[:, :, None] == slot_ids[None, None, :]) & is_valid[:, :, None]).astype(jnp.float32)

    def gather_rows(matrix):
        return jnp.einsum("csr,crd->csd", chooser, matrix.reshape(blocks, ROWS, -1).astype(jnp.float32)).reshape(SEQ, -1)

    def scatter_rows(matrix):
        return jnp.einsum("csr,csd->crd", chooser, matrix.reshape(blocks, ROWS, -1).astype(jnp.float32), precision=lax.Precision.HIGHEST).reshape(SEQ, -1)

    block_start = (jnp.arange(blocks, dtype=jnp.int32) * ROWS)[:, None]
    position = jnp.where(is_valid, block_start + block_sel, -1).astype(jnp.int32).reshape(SEQ)
    query_sel = gather_rows(layer_queries)
    key_value = jnp.concatenate([gather_rows(layer_keys), gather_rows(layer_values)], 1)
    output, maxima, totals = forward(query_sel, key_value, position, position)
    attn_b = output.astype(jnp.bfloat16)
    updated = (layer_input.astype(jnp.float32) + scatter_rows(attn_b)).astype(jnp.bfloat16)
    out_grad = gather_rows(layer_cotangent)
    query_grad, pair_grad = backward(query_sel, key_value, position, position, output, maxima, totals, out_grad)
    pair_rows = scatter_rows(pair_grad)
    width = KV_HEADS * HEAD_DIM
    return updated, scatter_rows(query_grad).astype(jnp.bfloat16), pair_rows[:, :width].astype(jnp.bfloat16), pair_rows[:, width:].astype(jnp.bfloat16)


def reference(segment_input, queries, keys, values, cotangent, selected, counts):
    updated, query_grad, key_grad, value_grad = lax.map(lambda items: one_segment(*items), (segment_input, queries, keys, values, cotangent, selected, counts))
    next_input = jnp.concatenate([jnp.zeros_like(updated[:1]), updated[:-1]], 0)
    return next_input, query_grad, key_grad, value_grad
```

```python
import functools, math
import jax, jax.numpy as jnp
from jax import lax
from jax.experimental import pallas as pl
from jax.experimental.pallas import tpu as pltpu
from jax.sharding import PartitionSpec as P

HEAD = 128
GROUP = 8
ROWS = 128
SLOTS = 32
BLOCKS = 16
CHUNK = 512
TILE = 512
SCALE = HEAD ** -0.5
LOG2E = math.log2(math.e)
BF = jnp.bfloat16
F32 = jnp.float32


def dot(a, b):
    return jnp.dot(a, b, preferred_element_type=F32)


def fold(x, op):
    return op(x.reshape(x.shape[0] // 8, 8, x.shape[1]), axis=0)


def block_pass(q, g, width, k_ref, v_ref, kt_ref, vt_ref, dk_ref, dv_ref, chunks, full, mask_of, scr):
    qs, gs, qt, gt, s_scr, e_scr, m_scr, l_scr, acc, dqa = scr
    cols = width * GROUP
    for h in range(GROUP):
        qh, gh = q[:, h * HEAD:(h + 1) * HEAD], g[:, h * HEAD:(h + 1) * HEAD]
        rows = slice(h * width, (h + 1) * width)
        qs[rows, :] = qh
        gs[rows, :] = gh
    for t in range(cols // 128):
        rows = slice(t * 128, (t + 1) * 128)
        qt[:, rows] = qs[rows, :].T
        gt[:, rows] = gs[rows, :].T
    tile = min(TILE, cols)
    tiles = [slice(t, t + tile) for t in range(0, cols, tile)]
    m_scr[:, :cols] = jnp.full((8, cols), -1e30, F32)
    l_scr[:, :cols] = jnp.zeros((8, cols), F32)
    acc[:, :cols] = jnp.zeros((HEAD, cols), F32)
    dqa[:, :cols] = jnp.zeros((HEAD, cols), F32)

    def at(c):
        return pl.ds(pl.multiple_of(c * CHUNK, CHUNK), CHUNK)

    def score(c, masked):
        k = k_ref[at(c), :]
        for t in tiles:
            s = dot(k, qt[:, t])
            if masked:
                s = jnp.where(mask_of(c), s, -1e30)
            s_scr[at(c), t] = s
            m_scr[:, t] = jnp.maximum(m_scr[:, t], fold(s, jnp.max))

    def loop(fn):
        lax.fori_loop(0, chunks, lambda c, z: (fn(c), z)[1], 0)

    lax.fori_loop(0, full, lambda c, z: (score(c, False), z)[1], 0)
    lax.fori_loop(full, chunks, lambda c, z: (score(c, True), z)[1], 0)
    top = jnp.max(m_scr[:, :cols], axis=0, keepdims=True) * (SCALE * LOG2E)
    m_scr[:, :cols] = jnp.broadcast_to(top, (8, cols))

    def weigh(c):
        for t in tiles:
            e = jnp.exp2(s_scr[at(c), t] * (SCALE * LOG2E) - m_scr[0:1, t])
            l_scr[:, t] += fold(e, jnp.sum)
            eb = e.astype(BF)
            e_scr[at(c), t] = eb
            acc[:, t] += dot(vt_ref[c], eb)

    loop(weigh)
    inv = 1.0 / jnp.sum(l_scr[:, :cols], axis=0, keepdims=True)
    attn_t = acc[:, :cols] * inv
    acc[:, :cols] = attn_t
    delta = jnp.sum(attn_t * gt[:, :cols].astype(F32), axis=0, keepdims=True)
    l_scr[:, :cols] = jnp.broadcast_to(inv, (8, cols))
    m_scr[:, :cols] = jnp.broadcast_to(delta, (8, cols))

    def back(c):
        v = v_ref[at(c), :]
        dk = dk_ref[at(c), :]
        dv = dv_ref[at(c), :]
        for t in tiles:
            dp = dot(v, gt[:, t])
            p = e_scr[at(c), t].astype(F32) * l_scr[0:1, t]
            ds = (p * (dp - m_scr[0:1, t])).astype(BF)
            dv += dot(p.astype(BF), gs[t, :])
            dk += dot(ds, qs[t, :])
            dqa[:, t] += dot(kt_ref[c], ds)
        dk_ref[at(c), :] = dk
        dv_ref[at(c), :] = dv

    loop(back)


def emit(src, width, scale, out, row, col):
    for t in range(width * GROUP // 128):
        x = (src[:, t * 128:(t + 1) * 128] * scale).T.astype(BF)
        per = 128 // width
        for i in range(per):
            h = t * per + i
            out[row:row + width, col + h * HEAD:col + (h + 1) * HEAD] = x[i * width:(i + 1) * width, :]


def scratch(cols):
    return [
        pltpu.VMEM((cols, HEAD), BF), pltpu.VMEM((cols, HEAD), BF),
        pltpu.VMEM((HEAD, cols), BF), pltpu.VMEM((HEAD, cols), BF),
        pltpu.VMEM((BLOCKS * ROWS, cols), F32), pltpu.VMEM((BLOCKS * ROWS, cols), BF),
        pltpu.VMEM((8, cols), F32), pltpu.VMEM((8, cols), F32),
        pltpu.VMEM((HEAD, cols), F32), pltpu.VMEM((HEAD, cols), F32),
    ]


def chooser(sel):
    return (lax.broadcasted_iota(jnp.int32, (ROWS, ROWS), 0) == sel[0:1, :]).astype(F32)


def compact(sel):
    return chooser(sel).T[:SLOTS, :].astype(BF)


HALF = GROUP * HEAD
QG = 2 * HALF
KV = 2 * HEAD
DENSE = BLOCKS * ROWS
FEW = BLOCKS * SLOTS
SENT = ROWS + SLOTS
COUNT = 16
MARKED = SENT + COUNT
VMEM = pl.BlockSpec(memory_space=pltpu.VMEM)
SMEM = pl.BlockSpec(memory_space=pltpu.SMEM)
WHOLE = pltpu.CompilerParams(vmem_limit_bytes=60 << 20)
PARAMS = pltpu.CompilerParams(vmem_limit_bytes=20 << 20)
ANY = pl.BlockSpec(memory_space=pl.ANY)
SEL = pl.BlockSpec((1, ROWS), lambda i, info: (0, 0))


def pack_kernel(wide, info, a, b, a_in, b_in, sel, sel_in, *outs):
    def fill(out, dense, few, few_sel):
        pick = compact(few_sel)
        for side in range(2):
            cols = slice(side * wide, (side + 1) * wide)
            out[:ROWS, cols] = dense[side][...]
            out[ROWS:SENT, cols] = dot(pick, few[side][...]).astype(BF)
        if out.shape[0] > SENT:
            count = jnp.sum((few_sel[0:1, :] >= 0).astype(F32), axis=1, keepdims=True)
            out[SENT:, :] = jnp.broadcast_to(count, (COUNT, 2 * wide)).astype(BF)

    for step, out in enumerate(outs):
        @pl.when(pl.program_id(0) == step)
        def _(out=out):
            @pl.when(info[0] == 1)
            def _():
                fill(out, (a, b), (a_in, b_in), sel_in)

            @pl.when(info[0] == 0)
            def _():
                fill(out, (a_in, b_in), (a, b), sel)


def pack(wide, rows, info, a, b, a_in, b_in, sel, sel_in):
    part = pl.BlockSpec((ROWS, wide), lambda i, info: (0, 2 * lax.rem(info[1] + i, 4) + info[0]))
    return list(pl.pallas_call(
        functools.partial(pack_kernel, wide),
        grid_spec=pltpu.PrefetchScalarGridSpec(
            num_scalar_prefetch=1,
            grid=(4,),
            in_specs=[part] * 4 + [SEL] * 2,
            out_specs=[pl.BlockSpec((rows, 2 * wide), lambda i, info: (0, 0))] * 4,
        ),
        out_shape=[jax.ShapeDtypeStruct((rows, 2 * wide), BF)] * 4,
        compiler_params=WHOLE,
        name="pack",
    )(info, a, b, a_in, b_in, sel, sel_in))


ATTEND = pltpu.CompilerParams(vmem_limit_bytes=32 << 20)
KEYED = [((DENSE, HEAD), BF)] * 2 + [((DENSE // CHUNK, HEAD, CHUNK), BF)] * 2
KEYED += [((FEW, HEAD), BF)] * 2 + [((FEW // CHUNK, HEAD, CHUNK), BF)] * 2 + [((FEW, HEAD), F32)]
SUMS = [((DENSE, HEAD), F32)] * 2 + [((FEW, HEAD), F32)] * 2


def cost(blocks):
    return pl.CostEstimate(flops=blocks * 9 * 10 ** 9, bytes_accessed=6 << 20, transcendentals=0)


def arrange(info, kvs, keyed):
    kd, vd, ktd, vtd, kr, vr, ktr, vtr, flags = keyed
    slot = lax.broadcasted_iota(jnp.int32, (SLOTS, HEAD), 0).astype(F32)
    for ky, kv in enumerate(kvs):
        for kz in range(4):
            b = 4 * lax.rem(info[1] + 4 - kz, 4) + lax.rem(info[2] + 4 - ky, 4)
            big = pl.ds(pl.multiple_of(b * ROWS, ROWS), ROWS)
            small = pl.ds(pl.multiple_of(b * SLOTS, SLOTS), SLOTS)
            kd[big, :] = kv[kz, :ROWS, :HEAD]
            vd[big, :] = kv[kz, :ROWS, HEAD:]
            kr[small, :] = kv[kz, ROWS:SENT, :HEAD]
            vr[small, :] = kv[kz, ROWS:SENT, HEAD:]
            flags[small, :] = (slot < kv[kz, SENT:, :HEAD].astype(F32)[0:1, :]).astype(F32)
    for k, v, kt, vt in ((kd, vd, ktd, vtd), (kr, vr, ktr, vtr)):
        for c in range(kt.shape[0]):
            rows = slice(c * CHUNK, (c + 1) * CHUNK)
            kt[c] = k[rows, :].T
            vt[c] = v[rows, :].T


def attend_block(info, shift, qg, keyed, sums, out, scr):
    kd, vd, ktd, vtd, kr, vr, ktr, vtr, flags = keyed
    per = CHUNK // ROWS
    blk = 4 * lax.rem(info[1] + 4 - shift, 4) + info[2]
    chunks = lax.div(blk + per, per)

    def place(cols):
        shape = (CHUNK, cols)
        return lax.broadcasted_iota(jnp.int32, shape, 0), lax.broadcasted_iota(jnp.int32, shape, 1)

    def causal(c):
        row, col = place(TILE)
        return c * CHUNK + row <= blk * ROWS + lax.rem(col, ROWS)

    def routed(c):
        cols = SLOTS * GROUP
        row, col = place(cols)
        near = c * CHUNK + row <= blk * SLOTS + lax.rem(col, SLOTS)
        held = flags[pl.ds(pl.multiple_of(c * CHUNK, CHUNK), CHUNK), :]
        return near & (jnp.concatenate([held] * (cols // HEAD), axis=1) > 0.5)

    block_pass(qg[:ROWS, :HALF], qg[:ROWS, HALF:], ROWS, kd, vd, ktd, vtd, sums[0], sums[1],
               chunks, chunks - 1, causal, scr)
    emit(scr[8], ROWS, 1.0, out, 0, 0)
    emit(scr[9], ROWS, SCALE, out, 0, HALF)
    block_pass(qg[ROWS:, :HALF], qg[ROWS:, HALF:], SLOTS, kr, vr, ktr, vtr, sums[2], sums[3],
               FEW // CHUNK, 0, routed, scr)
    emit(scr[8], SLOTS, 1.0, out, ROWS, 0)
    emit(scr[9], SLOTS, SCALE, out, ROWS, HALF)


def first_kernel(info, qg, kv0, kv1, kv2, kv3, out, *refs):
    keyed, sums, scr = refs[:9], refs[9:13], refs[13:]
    arrange(info, (kv0, kv1, kv2, kv3), keyed)
    for total in sums:
        total[...] = jnp.zeros_like(total)
    attend_block(info, 0, qg, keyed, sums, out, scr)


def attend_first(info, qg, kvs):
    shapes = [((SENT, QG), BF)] + KEYED + SUMS
    outs = pl.pallas_call(
        first_kernel,
        out_shape=[jax.ShapeDtypeStruct(s, d) for s, d in shapes],
        in_specs=[SMEM] + [VMEM] * 5,
        out_specs=[VMEM] * len(shapes),
        scratch_shapes=scratch(HALF),
        compiler_params=ATTEND,
        cost_estimate=cost(1),
        name="attend_first",
    )(info, qg, *kvs)
    return outs[0], outs[1:10], outs[10:]


def middle_kernel(shifts, info, *refs):
    n = len(shifts)
    qgs, refs = refs[:n], refs[n:]
    keyed, sums_in, refs = refs[:9], refs[9:13], refs[13:]
    outs, sums, scr = refs[:n], refs[n:n + 4], refs[n + 4:]
    for total, come in zip(sums, sums_in):
        total[...] = come[...]
    for shift, qg, out in zip(shifts, qgs, outs):
        attend_block(info, shift, qg, keyed, sums, out, scr)


def attend_middle(shifts, info, qgs, keyed, sums):
    n = len(shifts)
    shapes = [((SENT, QG), BF)] * n + SUMS
    outs = pl.pallas_call(
        functools.partial(middle_kernel, shifts),
        out_shape=[jax.ShapeDtypeStruct(s, d) for s, d in shapes],
        in_specs=[SMEM] + [VMEM] * (n + 13),
        out_specs=[VMEM] * len(shapes),
        scratch_shapes=scratch(HALF),
        input_output_aliases={n + 10 + i: n + i for i in range(4)},
        compiler_params=ATTEND,
        cost_estimate=cost(n),
        name="attend_middle",
    )(info, *qgs, *keyed, *sums)
    return outs[:n], outs[n:]


def last_kernel(shift, info, qg, *refs):
    keyed, sums_in, refs = refs[:9], refs[9:13], refs[13:]
    out, sent, sums, scr = refs[0], refs[1:5], refs[5:9], refs[9:]
    for total, come in zip(sums, sums_in):
        total[...] = come[...]
    attend_block(info, shift, qg, keyed, sums, out, scr)
    for ky in range(4):
        for kz in range(4):
            b = 4 * lax.rem(info[1] + kz, 4) + lax.rem(info[2] + ky, 4)
            big = pl.ds(pl.multiple_of(b * ROWS, ROWS), ROWS)
            small = pl.ds(pl.multiple_of(b * SLOTS, SLOTS), SLOTS)
            sent[ky][kz, :ROWS, :HEAD] = (sums[0][big, :] * SCALE).astype(BF)
            sent[ky][kz, :ROWS, HEAD:] = sums[1][big, :].astype(BF)
            sent[ky][kz, ROWS:, :HEAD] = (sums[2][small, :] * SCALE).astype(BF)
            sent[ky][kz, ROWS:, HEAD:] = sums[3][small, :].astype(BF)


def attend_last(shift, info, qg, keyed, sums):
    shapes = [(SENT, QG)] + [(4, SENT, KV)] * 4
    outs = pl.pallas_call(
        functools.partial(last_kernel, shift),
        out_shape=[jax.ShapeDtypeStruct(s, BF) for s in shapes],
        in_specs=[SMEM] + [VMEM] * 14,
        out_specs=[VMEM] * len(shapes),
        scratch_shapes=[pltpu.VMEM(s, d) for s, d in SUMS] + scratch(HALF),
        compiler_params=ATTEND,
        cost_estimate=cost(1),
        name="attend_last",
    )(info, qg, *keyed, *sums)
    return outs[0], list(outs[1:])


def fold_kernel(a, b, c, d, *outs):
    for i, out in enumerate(outs):
        total = a[i].astype(F32) + b[i].astype(F32) + c[i].astype(F32) + d[i].astype(F32)
        out[...] = total.astype(BF)


def fold_sums(parts):
    return list(pl.pallas_call(
        fold_kernel,
        out_shape=[jax.ShapeDtypeStruct((SENT, KV), BF)] * 4,
        in_specs=[VMEM] * 4,
        out_specs=[VMEM] * 4,
        compiler_params=PARAMS,
        name="fold_sums",
    )(*parts))


def heads_of(info, sel, mine, theirs, put):
    @pl.when(info[0] == 1)
    def _():
        put(0, theirs[0, :ROWS, :].astype(F32))
        put(1, mine[0, :ROWS, :].astype(F32))

    @pl.when(info[0] == 0)
    def _():
        pick = chooser(sel)[:, :SLOTS].astype(BF)
        put(0, dot(pick, mine[0, ROWS:, :]))
        put(1, dot(pick, theirs[0, ROWS:, :]))


def update_kernel(info, seg, mine, theirs, sel, out):
    def put(i, x):
        cols = slice(i * HALF, (i + 1) * HALF)
        out[0, :, cols] = (seg[:, cols].astype(F32) + x).astype(BF)

    heads_of(info, sel, mine, theirs, put)


def turner(shifts):
    def turn(i, info):
        shift = shifts[0]
        for j in range(1, len(shifts)):
            shift = jnp.where(i == j, shifts[j], shift)
        return lax.rem(info[1] + shift, 4)

    return turn


def update(shifts, info, seg, mine, theirs, sel):
    turn = turner(shifts)
    part = pl.BlockSpec((1, SENT, HALF), lambda i, info: (i, 0, 0))
    return pl.pallas_call(
        update_kernel,
        grid_spec=pltpu.PrefetchScalarGridSpec(
            num_scalar_prefetch=1,
            grid=(len(shifts),),
            in_specs=[pl.BlockSpec((ROWS, 2 * HALF), lambda i, info: (0, turn(i, info))), part, part, SEL],
            out_specs=pl.BlockSpec((1, ROWS, 2 * HALF), lambda i, info: (i, 0, 0)),
        ),
        out_shape=jax.ShapeDtypeStruct((len(shifts), ROWS, 2 * HALF), BF),
        compiler_params=PARAMS,
        name="update",
    )(info, seg, mine, theirs, sel)


def finish_kernel(info, near, near_in, far, far_in, sums, sums_in, sel, dq, dk, dv):
    def put_q(i, x):
        dq[:, i * HALF:(i + 1) * HALF] = x.astype(BF)

    def put_kv(i, x):
        x = x.astype(BF)
        dk[:, i * HEAD:(i + 1) * HEAD] = x[:, :HEAD]
        dv[:, i * HEAD:(i + 1) * HEAD] = x[:, HEAD:]

    @pl.when(pl.program_id(0) < 3)
    def _():
        heads_of(info, sel, near, near_in, put_q)

    @pl.when(pl.program_id(0) == 3)
    def _():
        heads_of(info, sel, far, far_in, put_q)

    heads_of(info, sel, sums, sums_in, put_kv)


def finish(info, near, near_in, far, far_in, sums, sums_in, sel):
    turn = turner((0, 1, 3, 2))

    def head(i, info):
        return (0, turn(i, info))

    def back(i, info):
        return (lax.rem(4 - turner((0, 1, 3, 2))(i, (0, 0)), 4), 0, 0)

    one = pl.BlockSpec((1, SENT, HALF), lambda i, info: (jnp.minimum(i, 2), 0, 1))
    two = pl.BlockSpec((1, SENT, HALF), lambda i, info: (0, 0, 1))
    tally = pl.BlockSpec((1, SENT, KV), back)
    return pl.pallas_call(
        finish_kernel,
        grid_spec=pltpu.PrefetchScalarGridSpec(
            num_scalar_prefetch=1,
            grid=(4,),
            in_specs=[one, one, two, two, tally, tally, SEL],
            out_specs=[
                pl.BlockSpec((ROWS, 2 * HALF), head),
                pl.BlockSpec((ROWS, 2 * HEAD), head),
                pl.BlockSpec((ROWS, 2 * HEAD), head),
            ],
        ),
        out_shape=[
            jax.ShapeDtypeStruct((ROWS, 8 * HALF), BF),
            jax.ShapeDtypeStruct((ROWS, 8 * HEAD), BF),
            jax.ShapeDtypeStruct((ROWS, 8 * HEAD), BF),
        ],
        compiler_params=PARAMS,
        name="finish",
    )(info, near, near_in, far, far_in, sums, sums_in, sel)


def join_kernel(info, near, far, out):
    out[...] = jnp.where(pl.program_id(0) == 3, far[0], near[0])


def join(info, near, far):
    def head(i, info):
        shift = jnp.where(i == 3, 2, jnp.where(i == 2, 3, i))
        return (0, lax.rem(info[1] + shift, 4))

    return pl.pallas_call(
        join_kernel,
        grid_spec=pltpu.PrefetchScalarGridSpec(
            num_scalar_prefetch=1,
            grid=(4,),
            in_specs=[
                pl.BlockSpec((1, ROWS, 2 * HALF), lambda i, info: (jnp.minimum(i, 2), 0, 0)),
                pl.BlockSpec((1, ROWS, 2 * HALF), lambda i, info: (0, 0, 0)),
            ],
            out_specs=pl.BlockSpec((ROWS, 2 * HALF), head),
        ),
        out_shape=jax.ShapeDtypeStruct((ROWS, 8 * HALF), BF),
        compiler_params=PARAMS,
        name="join",
    )(info, near, far)


def along_z(x, by):
    return lax.ppermute(x, "ctx", [(4 * z + y, 4 * ((z + by) % 4) + y) for z in range(4) for y in range(4)])


def along_y(x, by):
    return lax.ppermute(x, "ctx", [(4 * z + y, 4 * z + (y + by) % 4) for z in range(4) for y in range(4)])


def swap(x):
    return lax.ppermute(x, "section", [(i, i ^ 1) for i in range(8)])


def onward(x):
    return lax.ppermute(x, "section", [(i, i + 1) for i in range(7)])


def both(*xs):
    return lax.optimization_barrier(xs)


def body(segment_input, queries, keys, values, cotangent, selected, counts):
    section, place = lax.axis_index("section"), lax.axis_index("ctx")
    info = jnp.stack([section % 2, place // 4, place % 4]).astype(jnp.int32)
    seg, q, k, v, g = (x[0] for x in (segment_input, queries, keys, values, cotangent))
    sel = jnp.where(jnp.arange(ROWS, dtype=jnp.int32)[None, :] < counts, selected, -1)

    sel_in = swap(sel)
    kv = pack(HEAD, MARKED, info, k, v, swap(k), swap(v), sel, sel_in)
    for by in (1, 3, 2):
        kv[by] = along_z(kv[by], by)
    column = jnp.stack(kv)
    kvs = [column] + [along_y(column, by) for by in (1, 2, 3)]
    qg = pack(HALF, SENT, info, q, g, swap(q), swap(g), sel, sel_in)
    qg[1], qg[2], qg[3], _ = both(qg[1], qg[2], qg[3], column)
    for by in (1, 3, 2):
        qg[by] = along_z(qg[by], by)

    out = [None] * 4
    out[0], keyed, sums = attend_first(info, qg[0], kvs)
    (out[1], out[3]), sums = attend_middle((1, 3), info, [qg[1], qg[3]], keyed, sums)
    out[2], sent = attend_last(2, info, qg[2], keyed, sums)
    for by in (1, 3):
        out[by] = along_z(out[by], 4 - by)
    out[1], out[3], out[2] = both(out[1], out[3], out[2])
    out[2] = along_z(out[2], 2)
    sums = fold_sums([sent[0]] + [along_y(sent[by], by) for by in (1, 2, 3)])
    out[2], sums[0], sums[1], sums[2], sums[3] = both(out[2], *sums)

    near = jnp.stack([out[0], out[1], out[3]])
    near_in = swap(near)
    first = update((0, 1, 3), info, seg, near, near_in, sel)
    far = out[2][None]
    far_in = swap(far)
    second = update((2,), info, seg, far, far_in, sel)
    next_input = join(info, onward(first), onward(second))

    sums = jnp.stack([sums[0]] + [along_z(sums[by], by) for by in (1, 2, 3)])
    grads = finish(info, near, near_in, far, far_in, sums, swap(sums), sel)
    return (next_input[None],) + tuple(x[None] for x in grads)


def solution(mesh):
    wide, thin = P("section", "ctx", None), P("section", "ctx")
    return jax.shard_map(
        body,
        mesh=mesh,
        in_specs=(wide,) * 5 + (thin,) * 2,
        out_specs=(wide,) * 4,
        check_vma=False,
    )
```

```python
import functools, math
import jax, jax.numpy as jnp
from jax import lax
from jax.experimental import pallas as pl
from jax.experimental.pallas import tpu as pltpu
from jax.sharding import PartitionSpec as P

HEAD = 128
GROUP = 8
ROWS = 128
SLOTS = 32
BLOCKS = 16
CHUNK = 512
TILE = 512
SCALE = HEAD ** -0.5
LOG2E = math.log2(math.e)
BF = jnp.bfloat16
F32 = jnp.float32


def dot(a, b):
    return jnp.dot(a, b, preferred_element_type=F32)


def fold(x, op):
    return op(x.reshape(x.shape[0] // 8, 8, x.shape[1]), axis=0)


def turned(x, width, rows, out):
    cols = width * GROUP
    for h in range(GROUP):
        rows[h * width:(h + 1) * width, :] = x[:, h * HEAD:(h + 1) * HEAD]
    for t in range(0, cols, HEAD):
        out[:, t:t + HEAD] = rows[t:t + HEAD, :].T


def tiles_of(cols):
    tile = min(TILE, cols)
    return [slice(t, t + tile) for t in range(0, cols, tile)]


def at(c):
    return pl.ds(pl.multiple_of(c * CHUNK, CHUNK), CHUNK)


def loop(first, end, fn):
    lax.fori_loop(first, end, lambda c, z: (fn(c), z)[1], 0)


def forward_pass(q, width, k_ref, vt_ref, e_ref, stat, acc, chunks, full, mask_of, scr):
    rows, qt, s_scr, m_scr, l_scr = scr
    cols = width * GROUP
    turned(q, width, rows, qt)
    tiles = tiles_of(cols)
    m_scr[:, :cols] = jnp.full((8, cols), -1e30, F32)
    l_scr[:, :cols] = jnp.zeros((8, cols), F32)
    acc[...] = jnp.zeros((HEAD, cols), F32)

    def score(c, masked):
        k = k_ref[at(c), :]
        for t in tiles:
            s = dot(k, qt[:, t])
            if masked:
                s = jnp.where(mask_of(c), s, -1e30)
            s_scr[at(c), t] = s
            m_scr[:, t] = jnp.maximum(m_scr[:, t], fold(s, jnp.max))

    loop(0, full, lambda c: score(c, False))
    loop(full, chunks, lambda c: score(c, True))
    top = jnp.max(m_scr[:, :cols], axis=0, keepdims=True) * (SCALE * LOG2E)
    m_scr[:, :cols] = jnp.broadcast_to(top, (8, cols))

    def weigh(c):
        for t in tiles:
            e = jnp.exp2(s_scr[at(c), t] * (SCALE * LOG2E) - m_scr[0:1, t])
            l_scr[:, t] += fold(e, jnp.sum)
            eb = e.astype(BF)
            e_ref[at(c), t] = eb
            acc[:, t] += dot(vt_ref[c], eb)

    loop(0, chunks, weigh)
    inv = 1.0 / jnp.sum(l_scr[:, :cols], axis=0, keepdims=True)
    acc[:, :cols] = acc[:, :cols] * inv
    stat[...] = jnp.broadcast_to(inv, (8, cols))


def backward_pass(q, g, width, v_ref, kt_ref, e_ref, stat, attn_t, dk_ref, dv_ref, chunks, scr):
    qs, gs, gt, acc, d_scr = scr
    cols = width * GROUP
    for h in range(GROUP):
        qs[h * width:(h + 1) * width, :] = q[:, h * HEAD:(h + 1) * HEAD]
    turned(g, width, gs, gt)
    tiles = tiles_of(cols)
    acc[:, :cols] = jnp.zeros((HEAD, cols), F32)
    delta = jnp.sum(attn_t[...] * gt[:, :cols].astype(F32), axis=0, keepdims=True)
    d_scr[:, :cols] = jnp.broadcast_to(delta, (8, cols))

    def back(c):
        v = v_ref[at(c), :]
        dk = dk_ref[at(c), :]
        dv = dv_ref[at(c), :]
        for t in tiles:
            dp = dot(v, gt[:, t])
            p = e_ref[at(c), t].astype(F32) * stat[0:1, t]
            ds = (p * (dp - d_scr[0:1, t])).astype(BF)
            dv += dot(p.astype(BF), gs[t, :])
            dk += dot(ds, qs[t, :])
            acc[:, t] += dot(kt_ref[c], ds)
        dk_ref[at(c), :] = dk
        dv_ref[at(c), :] = dv

    loop(0, chunks, back)


def emit(src, width, scale, out, row, col):
    for t in range(width * GROUP // 128):
        x = (src[:, t * 128:(t + 1) * 128] * scale).T.astype(BF)
        per = 128 // width
        for i in range(per):
            h = t * per + i
            out[row:row + width, col + h * HEAD:col + (h + 1) * HEAD] = x[i * width:(i + 1) * width, :]


def chooser(sel):
    return (lax.broadcasted_iota(jnp.int32, (ROWS, ROWS), 0) == sel[0:1, :]).astype(F32)


def compact(sel):
    return chooser(sel).T[:SLOTS, :].astype(BF)


HALF = GROUP * HEAD
QG = 2 * HALF
KV = 2 * HEAD
DENSE = BLOCKS * ROWS
FEW = BLOCKS * SLOTS
SENT = ROWS + SLOTS
COUNT = 16
MARKED = SENT + COUNT
VMEM = pl.BlockSpec(memory_space=pltpu.VMEM)
SMEM = pl.BlockSpec(memory_space=pltpu.SMEM)
WHOLE = pltpu.CompilerParams(vmem_limit_bytes=60 << 20)
PARAMS = pltpu.CompilerParams(vmem_limit_bytes=16 << 20)
ANY = pl.BlockSpec(memory_space=pl.ANY)
SEL = pl.BlockSpec((1, ROWS), lambda i, info: (0, 0))


def own_head(shift):
    core, z = lax.rem(lax.axis_index("section"), 2), lax.div(lax.axis_index("ctx"), 4)
    return 2 * lax.rem(z + shift, 4) + core, core


def pack_kv_kernel(k, v, k_in, v_in, sel, sel_in, *outs):
    def fill(dense, few, few_sel):
        pick = compact(few_sel)
        count = jnp.sum((few_sel[0:1, :] >= 0).astype(F32), axis=1, keepdims=True)
        for step, out in enumerate(outs):
            here = pl.ds(pl.multiple_of(own_head(step)[0] * HEAD, HEAD), HEAD)
            for side in range(2):
                cols = slice(side * HEAD, (side + 1) * HEAD)
                out[:ROWS, cols] = dense[side][:, here]
                out[ROWS:SENT, cols] = dot(pick, few[side][:, here]).astype(BF)
            out[SENT:, :] = jnp.broadcast_to(count, (COUNT, KV)).astype(BF)

    @pl.when(own_head(0)[1] == 1)
    def _():
        fill((k, v), (k_in, v_in), sel_in)

    @pl.when(own_head(0)[1] == 0)
    def _():
        fill((k_in, v_in), (k, v), sel)


def pack_kv(k, v, k_in, v_in, sel, sel_in):
    return list(pl.pallas_call(
        pack_kv_kernel,
        out_shape=[jax.ShapeDtypeStruct((MARKED, KV), BF)] * 4,
        in_specs=[VMEM] * 6,
        out_specs=[VMEM] * 4,
        compiler_params=PARAMS,
        name="pack_kv",
    )(k, v, k_in, v_in, sel, sel_in))


def pack_kernel(own, come, sel, sel_in, o0, o1, o2, o3, held, sems):
    core = own_head(0)[1]
    outs, copies = (o0, o1, o2, o3), []
    for step in range(4):
        here = pl.ds(pl.multiple_of(own_head(step)[0] * HALF, HALF), HALF)
        for i, ref in enumerate((own, come)):
            copies.append(pltpu.make_async_copy(ref.at[:, here], held.at[step, i], sems.at[2 * step + i]))
            copies[-1].start()
    pick = compact(jnp.where(core == 1, sel_in[...], sel[...]))
    for step, out in enumerate(outs):
        copies[2 * step].wait()
        copies[2 * step + 1].wait()

        @pl.when(core == 1)
        def _(step=step, out=out):
            out[:ROWS, :] = held[step, 0]
            out[ROWS:, :] = dot(pick, held[step, 1]).astype(BF)

        @pl.when(core == 0)
        def _(step=step, out=out):
            out[:ROWS, :] = held[step, 1]
            out[ROWS:, :] = dot(pick, held[step, 0]).astype(BF)


def pack(own, come, sel, sel_in):
    return list(pl.pallas_call(
        pack_kernel,
        out_shape=[jax.ShapeDtypeStruct((SENT, HALF), BF)] * 4,
        in_specs=[ANY] * 2 + [VMEM] * 2,
        out_specs=[VMEM] * 4,
        scratch_shapes=[pltpu.VMEM((4, 2, ROWS, HALF), BF), pltpu.SemaphoreType.DMA((8,))],
        compiler_params=WHOLE,
        name="pack",
    )(own, come, sel, sel_in))


FORTH = pltpu.CompilerParams(vmem_limit_bytes=12 << 20)
BACK = pltpu.CompilerParams(vmem_limit_bytes=8 << 20)
SUMS = [((DENSE, HEAD), F32)] * 2 + [((FEW, HEAD), F32)] * 2
FEWER = SLOTS * GROUP
LEFT = [((SENT, HALF), BF), ((DENSE, HALF), BF), ((8, HALF), F32), ((HEAD, HALF), F32),
        ((FEW, FEWER), BF), ((8, FEWER), F32), ((HEAD, FEWER), F32)]
KEYS = [((DENSE, HEAD), BF), ((DENSE // CHUNK, HEAD, CHUNK), BF), ((FEW, HEAD), BF), ((FEW // CHUNK, HEAD, CHUNK), BF)]
KEYED = KEYS + KEYS + [((FEW, HEAD), F32)]


def shaped(shapes):
    return [jax.ShapeDtypeStruct(s, d) for s, d in shapes]


def held(shapes):
    return [pltpu.VMEM(s, d) for s, d in shapes]


FORWARD = held([((HALF, HEAD), BF), ((HEAD, HALF), BF), ((DENSE, HALF), F32), ((8, HALF), F32), ((8, HALF), F32)])
BACKWARD = held([((HALF, HEAD), BF), ((HALF, HEAD), BF), ((HEAD, HALF), BF), ((HEAD, HALF), F32), ((8, HALF), F32)])


def cost(flops):
    return pl.CostEstimate(flops=int(flops), bytes_accessed=4 << 20, transcendentals=0)


def turn_blocks(x, xt):
    for c in range(xt.shape[0]):
        xt[c] = x[c * CHUNK:(c + 1) * CHUNK, :].T


def arrange(info, kvs, keyed):
    kd, ktd, kr, ktr, vd, vtd, vr, vtr, flags = keyed
    slot = lax.broadcasted_iota(jnp.int32, (SLOTS, HEAD), 0).astype(F32)
    for ky, kv in enumerate(kvs):
        for kz in range(4):
            b = 4 * lax.rem(info[1] + 4 - kz, 4) + lax.rem(info[2] + 4 - ky, 4)
            big = pl.ds(pl.multiple_of(b * ROWS, ROWS), ROWS)
            small = pl.ds(pl.multiple_of(b * SLOTS, SLOTS), SLOTS)
            kd[big, :] = kv[kz, :ROWS, :HEAD]
            vd[big, :] = kv[kz, :ROWS, HEAD:]
            kr[small, :] = kv[kz, ROWS:SENT, :HEAD]
            vr[small, :] = kv[kz, ROWS:SENT, HEAD:]
            flags[small, :] = (slot < kv[kz, SENT:, :HEAD].astype(F32)[0:1, :]).astype(F32)
    for x, xt in ((kd, ktd), (kr, ktr), (vd, vtd), (vr, vtr)):
        turn_blocks(x, xt)


def reach(info, shift):
    blk = 4 * lax.rem(info[1] + 4 - shift, 4) + info[2]
    per = CHUNK // ROWS
    return blk, lax.div(blk + per, per)


def forward_block(info, shift, q, keyed, left, scr):
    kd, _, kr, _, _, vtd, _, vtr, flags = keyed
    attn, e_dense, inv_dense, t_dense, e_few, inv_few, t_few = left
    blk, chunks = reach(info, shift)

    def place(cols):
        shape = (CHUNK, cols)
        return lax.broadcasted_iota(jnp.int32, shape, 0), lax.broadcasted_iota(jnp.int32, shape, 1)

    def causal(c):
        row, col = place(TILE)
        return c * CHUNK + row <= blk * ROWS + lax.rem(col, ROWS)

    def routed(c):
        row, col = place(FEWER)
        near = c * CHUNK + row <= blk * SLOTS + lax.rem(col, SLOTS)
        return near & (jnp.concatenate([flags[at(c), :]] * (FEWER // HEAD), axis=1) > 0.5)

    forward_pass(q[:ROWS, :], ROWS, kd, vtd, e_dense, inv_dense, t_dense, chunks, chunks - 1, causal, scr)
    emit(t_dense, ROWS, 1.0, attn, 0, 0)
    forward_pass(q[ROWS:, :], SLOTS, kr, vtr, e_few, inv_few, t_few, FEW // CHUNK, 0, routed, scr)
    emit(t_few, SLOTS, 1.0, attn, ROWS, 0)


def forward_kernel(shifts, first, info, *refs):
    n, m = len(shifts), len(LEFT)
    qs, refs = refs[:n], refs[n:]
    if first:
        kvs, refs = refs[:4], refs[4:]
    else:
        keyed, refs = refs[:9], refs[9:]
    lefts, refs = refs[:m * n], refs[m * n:]
    if first:
        keyed, refs = refs[:9], refs[9:]
        arrange(info, kvs, keyed)
    for i, shift in enumerate(shifts):
        forward_block(info, shift, qs[i], keyed, lefts[m * i:m * (i + 1)], refs)


def forward(shifts, info, qs, kvs=None, keyed=None):
    n, m, first = len(shifts), len(LEFT), kvs is not None
    shapes = LEFT * n + (KEYED if first else [])
    others = list(kvs if first else keyed)
    outs = pl.pallas_call(
        functools.partial(forward_kernel, shifts, first),
        out_shape=shaped(shapes),
        in_specs=[SMEM] + [VMEM] * (n + len(others)),
        out_specs=[VMEM] * len(shapes),
        scratch_shapes=FORWARD,
        compiler_params=FORTH,
        cost_estimate=cost(n * 4e9),
        name="forward",
    )(info, *qs, *others)
    lefts = [list(outs[m * i:m * (i + 1)]) for i in range(n)]
    return (lefts, outs[m * n:]) if first else lefts


def backward_block(info, shift, q, g, keyed, left, sums, dq, scr):
    _, ktd, _, ktr, vd, _, vr, _, _ = keyed
    _, chunks = reach(info, shift)
    backward_pass(q[:ROWS, :], g[:ROWS, :], ROWS, vd, ktd, *left[:3], *sums[:2], chunks, scr)
    emit(scr[3], ROWS, SCALE, dq, 0, 0)
    backward_pass(q[ROWS:, :], g[ROWS:, :], SLOTS, vr, ktr, *left[3:], *sums[2:], FEW // CHUNK, scr)
    emit(scr[3], SLOTS, SCALE, dq, ROWS, 0)


def backward_kernel(shifts, first, info, *refs):
    n, m = len(shifts), len(LEFT) - 1
    qs, gs, refs = refs[:n], refs[n:2 * n], refs[2 * n:]
    lefts, keyed, refs = refs[:m * n], refs[m * n:m * n + 9], refs[m * n + 9:]
    if first:
        dqs, sums, scr = refs[:n], refs[n:n + 4], refs[n + 4:]
    else:
        came, dqs, sent, sums, scr = refs[:4], refs[4:n + 4], refs[n + 4:n + 8], refs[n + 8:n + 12], refs[n + 12:]
    for i, total in enumerate(sums):
        total[...] = jnp.zeros_like(total) if first else came[i][...]
    for i, shift in enumerate(shifts):
        backward_block(info, shift, qs[i], gs[i], keyed, lefts[m * i:m * (i + 1)], sums, dqs[i], scr)
    for ky in range(0 if first else 4):
        for kz in range(4):
            b = 4 * lax.rem(info[1] + kz, 4) + lax.rem(info[2] + ky, 4)
            big = pl.ds(pl.multiple_of(b * ROWS, ROWS), ROWS)
            small = pl.ds(pl.multiple_of(b * SLOTS, SLOTS), SLOTS)
            sent[ky][kz, :ROWS, :HEAD] = (sums[0][big, :] * SCALE).astype(BF)
            sent[ky][kz, :ROWS, HEAD:] = sums[1][big, :].astype(BF)
            sent[ky][kz, ROWS:, :HEAD] = (sums[2][small, :] * SCALE).astype(BF)
            sent[ky][kz, ROWS:, HEAD:] = sums[3][small, :].astype(BF)


def backward(shifts, info, qs, gs, lefts, keyed, sums=()):
    n, first = len(shifts), not sums
    shapes = [((SENT, HALF), BF)] * n + (SUMS if first else [((4, SENT, KV), BF)] * 4)
    args = [qs[i] for i in shifts] + [gs[i] for i in shifts] + [x for i in shifts for x in lefts[i][1:]]
    args += list(keyed) + list(sums)
    outs = pl.pallas_call(
        functools.partial(backward_kernel, shifts, first),
        out_shape=shaped(shapes),
        in_specs=[SMEM] + [VMEM] * len(args),
        out_specs=[VMEM] * len(shapes),
        scratch_shapes=([] if first else held(SUMS)) + BACKWARD,
        compiler_params=BACK,
        cost_estimate=cost(n * 6e9),
        name="backward",
    )(info, *args)
    return list(outs[:n]), list(outs[n:])


def fold_kernel(a, b, c, d, *outs):
    for i, out in enumerate(outs):
        total = a[i].astype(F32) + b[i].astype(F32) + c[i].astype(F32) + d[i].astype(F32)
        out[...] = total.astype(BF)


def fold_sums(parts):
    return list(pl.pallas_call(
        fold_kernel,
        out_shape=[jax.ShapeDtypeStruct((SENT, KV), BF)] * 4,
        in_specs=[VMEM] * 4,
        out_specs=[VMEM] * 4,
        compiler_params=PARAMS,
        name="fold_sums",
    )(*parts))


def heads_of(info, sel, mine, theirs, put):
    @pl.when(info[0] == 1)
    def _():
        put(0, theirs[0, :ROWS, :].astype(F32))
        put(1, mine[0, :ROWS, :].astype(F32))

    @pl.when(info[0] == 0)
    def _():
        pick = chooser(sel)[:, :SLOTS].astype(BF)
        put(0, dot(pick, mine[0, ROWS:, :]))
        put(1, dot(pick, theirs[0, ROWS:, :]))


def update_kernel(info, seg, mine, theirs, sel, out):
    def put(i, x):
        cols = slice(i * HALF, (i + 1) * HALF)
        out[:, cols] = (seg[:, cols].astype(F32) + x).astype(BF)

    heads_of(info, sel, mine, theirs, put)


def finish_q_kernel(info, mine, theirs, sel, out):
    def put(i, x):
        out[:, i * HALF:(i + 1) * HALF] = x.astype(BF)

    heads_of(info, sel, mine, theirs, put)


def by_head(kernel, name, info, seg, mine, theirs, sel):
    part = pl.BlockSpec((1, SENT, HALF), lambda i, info: (i, 0, 0))
    whole = pl.BlockSpec((ROWS, 2 * HALF), lambda i, info: (0, lax.rem(info[1] + i, 4)))
    segs = [] if seg is None else [seg]
    return pl.pallas_call(
        kernel,
        grid_spec=pltpu.PrefetchScalarGridSpec(
            num_scalar_prefetch=1,
            grid=(4,),
            in_specs=[whole] * len(segs) + [part, part, SEL],
            out_specs=whole,
        ),
        out_shape=jax.ShapeDtypeStruct((ROWS, 8 * HALF), BF),
        compiler_params=PARAMS,
        name=name,
    )(info, *segs, mine, theirs, sel)


def settle_kernel(x, out):
    out[...] = x[...]


def settle(x):
    part = pl.BlockSpec((ROWS, 2 * HALF), lambda i: (0, i))
    return pl.pallas_call(
        settle_kernel,
        grid=(4,),
        in_specs=[part],
        out_specs=part,
        out_shape=jax.ShapeDtypeStruct(x.shape, x.dtype),
        compiler_params=PARAMS,
        name="settle",
    )(x)


def finish_kv_kernel(info, sums, sums_in, sel, dk, dv):
    def fill(even, odd, rows):
        for shift in range(4):
            for i, ref in enumerate((even, odd)):
                head = 2 * lax.rem(info[1] + 4 - shift, 4) + i
                at = pl.ds(pl.multiple_of(head * HEAD, HEAD), HEAD)
                x = rows(ref[shift])
                dk[:, at] = x[:, :HEAD]
                dv[:, at] = x[:, HEAD:]

    @pl.when(info[0] == 1)
    def _():
        fill(sums_in, sums, lambda x: x[:ROWS, :])

    @pl.when(info[0] == 0)
    def _():
        pick = chooser(sel)[:, :SLOTS].astype(BF)
        fill(sums, sums_in, lambda x: dot(pick, x[ROWS:, :]).astype(BF))


def finish_kv(info, sums, sums_in, sel):
    return pl.pallas_call(
        finish_kv_kernel,
        out_shape=[jax.ShapeDtypeStruct((ROWS, 8 * HEAD), BF)] * 2,
        in_specs=[SMEM] + [VMEM] * 3,
        out_specs=[VMEM] * 2,
        compiler_params=PARAMS,
        name="finish_kv",
    )(info, sums, sums_in, sel)


def along_z(x, by):
    return lax.ppermute(x, "ctx", [(4 * z + y, 4 * ((z + by) % 4) + y) for z in range(4) for y in range(4)])


def along_y(x, by):
    return lax.ppermute(x, "ctx", [(4 * z + y, 4 * z + (y + by) % 4) for z in range(4) for y in range(4)])


def swap(x):
    return lax.ppermute(x, "section", [(i, i ^ 1) for i in range(8)])


def onward(x):
    return lax.ppermute(x, "section", [(i, i + 1) for i in range(7)])


def both(*xs):
    return lax.optimization_barrier(xs)


def body(segment_input, queries, keys, values, cotangent, selected, counts):
    section, place = lax.axis_index("section"), lax.axis_index("ctx")
    info = jnp.stack([section % 2, place // 4, place % 4]).astype(jnp.int32)
    seg, q, k, v, g = (x[0] for x in (segment_input, queries, keys, values, cotangent))
    sel = jnp.where(jnp.arange(ROWS, dtype=jnp.int32)[None, :] < counts, selected, -1)

    k_in, v_in, sel_in = swap(k), swap(v), swap(sel)
    kv = pack_kv(k, v, k_in, v_in, sel, sel_in)
    q, g, *_ = both(q, g, k_in, v_in, sel_in)
    q_in, g_in = swap(q), swap(g)
    qs = pack(q, q_in, sel, sel_in)
    for by in (1, 3, 2):
        kv[by] = along_z(kv[by], by)
    kv[1], kv[2], kv[3], qs[1], qs[2], qs[3], g_in = both(kv[1], kv[2], kv[3], qs[1], qs[2], qs[3], g_in)
    column = jnp.stack(kv)
    kvs = [column] + [along_y(column, by) for by in (1, 2, 3)]
    qs[1], qs[2], qs[3], g_in, _ = both(qs[1], qs[2], qs[3], g_in, column)
    for by in (1, 3, 2):
        qs[by] = along_z(qs[by], by)
    gs = pack(g, g_in, sel, sel_in)

    (own,), keyed = forward((0,), info, [qs[0]], kvs=kvs)
    for by in (1, 3, 2):
        gs[by] = along_z(gs[by], by)
    one, three, two = forward((1, 3, 2), info, [qs[1], qs[3], qs[2]], keyed=keyed)
    lefts = [own, one, two, three]
    attn = [along_z(lefts[by][0], 4 - by) if by else lefts[by][0] for by in range(4)]
    dq = [None] * 4
    (dq[1], dq[3]), sums = backward((1, 3), info, qs, gs, lefts, keyed)
    (dq[0], dq[2]), sent = backward((0, 2), info, qs, gs, lefts, keyed, sums)
    dq = [along_z(dq[by], 4 - by) if by else dq[by] for by in range(4)]
    attn[1], attn[2], attn[3], dq[1], dq[3], sent[0] = both(attn[1], attn[2], attn[3], dq[1], dq[3], sent[0])
    attn = jnp.stack(attn)
    updated = by_head(update_kernel, "update", info, seg, attn, swap(attn), sel)
    next_input = onward(updated)
    sums = fold_sums([sent[0]] + [along_y(sent[by], by) for by in (1, 2, 3)])
    dq[2], sums[0] = both(dq[2], sums[0])
    dq = jnp.stack(dq)
    query_grad = by_head(finish_q_kernel, "finish_q", info, None, dq, swap(dq), sel)
    sums = [sums[0]] + [along_z(sums[by], by) for by in (1, 2, 3)]
    next_input, query_grad, *sums = both(settle(next_input), query_grad, *sums)
    sums = jnp.stack(sums)
    key_grad, value_grad = finish_kv(info, sums, swap(sums), sel)
    return next_input[None], query_grad[None], key_grad[None], value_grad[None]


def solution(mesh):
    wide, thin = P("section", "ctx", None), P("section", "ctx")
    return jax.shard_map(
        body,
        mesh=mesh,
        in_specs=(wide,) * 5 + (thin,) * 2,
        out_specs=(wide,) * 4,
        check_vma=False,
    )
```

```python
import functools, math
import jax, jax.numpy as jnp
from jax import lax
from jax.experimental import pallas as pl
from jax.experimental.pallas import tpu as pltpu
from jax.sharding import PartitionSpec as P

HEAD = 128
GROUP = 8
ROWS = 128
SLOTS = 32
BLOCKS = 16
CHUNK = 512
TILE = 512
SCALE = HEAD ** -0.5
LOG2E = math.log2(math.e)
BF = jnp.bfloat16
F32 = jnp.float32


def dot(a, b):
    return jnp.dot(a, b, preferred_element_type=F32)


def fold(x, op):
    return op(x.reshape(x.shape[0] // 8, 8, x.shape[1]), axis=0)


def turned(x, width, rows, out):
    cols = width * GROUP
    for h in range(GROUP):
        rows[h * width:(h + 1) * width, :] = x[:, h * HEAD:(h + 1) * HEAD]
    for t in range(0, cols, HEAD):
        out[:, t:t + HEAD] = rows[t:t + HEAD, :].T


def tiles_of(cols, tile):
    tile = min(tile, cols)
    return [slice(t, t + tile) for t in range(0, cols, tile)]


def at(c):
    return pl.ds(pl.multiple_of(c * CHUNK, CHUNK), CHUNK)


def loop(first, end, fn):
    lax.fori_loop(first, end, lambda c, z: (fn(c), z)[1], 0)


def forward_pass(q, width, k_ref, vt_ref, e_ref, stat, acc, chunks, full, mask_of, scr):
    rows, qt, s_scr, m_scr, l_scr = scr
    cols = width * GROUP
    turned(q, width, rows, qt)
    tiles = tiles_of(cols, TILE)
    m_scr[:, :cols] = jnp.full((8, cols), -1e30, F32)
    l_scr[:, :cols] = jnp.zeros((8, cols), F32)
    acc[...] = jnp.zeros((HEAD, cols), F32)

    def score(c, masked):
        k = k_ref[at(c), :]
        for t in tiles:
            s = dot(k, qt[:, t])
            if masked:
                s = jnp.where(mask_of(c), s, -1e30)
            s_scr[at(c), t] = s
            m_scr[:, t] = jnp.maximum(m_scr[:, t], fold(s, jnp.max))

    loop(0, full, lambda c: score(c, False))
    loop(full, chunks, lambda c: score(c, True))
    top = jnp.max(m_scr[:, :cols], axis=0, keepdims=True) * (SCALE * LOG2E)
    m_scr[:, :cols] = jnp.broadcast_to(top, (8, cols))

    def weigh(c):
        for t in tiles:
            e = jnp.exp2(s_scr[at(c), t] * (SCALE * LOG2E) - m_scr[0:1, t])
            l_scr[:, t] += fold(e, jnp.sum)
            eb = e.astype(BF)
            e_ref[at(c), t] = eb
            acc[:, t] += dot(vt_ref[c], eb)

    loop(0, chunks, weigh)
    inv = 1.0 / jnp.sum(l_scr[:, :cols], axis=0, keepdims=True)
    acc[:, :cols] = acc[:, :cols] * inv
    stat[...] = jnp.broadcast_to(inv, (8, cols))


def backward_pass(q, g, width, v_ref, kt_ref, e_ref, stat, attn_t, dk_ref, dv_ref, chunks, scr):
    qs, gs, gt, acc, d_scr = scr
    cols = width * GROUP
    for h in range(GROUP):
        qs[h * width:(h + 1) * width, :] = q[:, h * HEAD:(h + 1) * HEAD]
    turned(g, width, gs, gt)
    for t in range(0, cols, HEAD):
        part = (gt[:, t:t + HEAD].astype(F32) * stat[0:1, t:t + HEAD]).astype(BF)
        gt[:, t:t + HEAD] = part
        gs[t:t + HEAD, :] = part.T
    tiles = tiles_of(cols, HALF)
    acc[:, :cols] = jnp.zeros((HEAD, cols), F32)
    delta = jnp.sum(attn_t[...] * gt[:, :cols].astype(F32), axis=0, keepdims=True)
    d_scr[:, :cols] = jnp.broadcast_to(delta, (8, cols))

    def back(c):
        v = v_ref[at(c), :]
        dk = dk_ref[at(c), :]
        dv = dv_ref[at(c), :]
        for t in tiles:
            e = e_ref[at(c), t]
            ds = (e.astype(F32) * (dot(v, gt[:, t]) - d_scr[0:1, t])).astype(BF)
            dv += dot(e, gs[t, :])
            dk += dot(ds, qs[t, :])
            acc[:, t] += dot(kt_ref[c], ds)
        dk_ref[at(c), :] = dk
        dv_ref[at(c), :] = dv

    loop(0, chunks, back)


def emit(src, width, scale, out, row, col):
    for t in range(width * GROUP // 128):
        x = (src[:, t * 128:(t + 1) * 128] * scale).T.astype(BF)
        per = 128 // width
        for i in range(per):
            h = t * per + i
            out[row:row + width, col + h * HEAD:col + (h + 1) * HEAD] = x[i * width:(i + 1) * width, :]


def chooser(sel):
    return (lax.broadcasted_iota(jnp.int32, (ROWS, ROWS), 0) == sel[0:1, :]).astype(F32)


def compact(sel):
    return chooser(sel).T[:SLOTS, :].astype(BF)


HALF = GROUP * HEAD
QG = 2 * HALF
KV = 2 * HEAD
DENSE = BLOCKS * ROWS
FEW = BLOCKS * SLOTS
SENT = ROWS + SLOTS
INVALID = 128.0
VMEM = pl.BlockSpec(memory_space=pltpu.VMEM)
SMEM = pl.BlockSpec(memory_space=pltpu.SMEM)
WHOLE = pltpu.CompilerParams(vmem_limit_bytes=60 << 20)
PARAMS = pltpu.CompilerParams(vmem_limit_bytes=16 << 20)
ANY = pl.BlockSpec(memory_space=pl.ANY)
SEL = pl.BlockSpec((1, ROWS), lambda i, info: (0, 0))


def own_head(shift):
    core, z = lax.rem(lax.axis_index("section"), 2), lax.div(lax.axis_index("ctx"), 4)
    return 2 * lax.rem(z + shift, 4) + core, core


def pack_kv_kernel(k, v, k_in, v_in, sel, sel_in, *outs):
    def fill(dense, few, few_sel):
        pick = compact(few_sel)
        mark = INVALID * (1.0 - jnp.sum(pick.astype(F32), axis=1, keepdims=True))
        for step, out in enumerate(outs):
            here = pl.ds(pl.multiple_of(own_head(step)[0] * HEAD, HEAD), HEAD)
            for side in range(2):
                cols = slice(side * HEAD, (side + 1) * HEAD)
                out[:ROWS, cols] = dense[side][:, here]
                rows = dot(pick, few[side][:, here])
                out[ROWS:, cols] = (rows if side else rows + mark).astype(BF)

    @pl.when(own_head(0)[1] == 1)
    def _():
        fill((k, v), (k_in, v_in), sel_in)

    @pl.when(own_head(0)[1] == 0)
    def _():
        fill((k_in, v_in), (k, v), sel)


def pack_kv(k, v, k_in, v_in, sel, sel_in):
    return list(pl.pallas_call(
        pack_kv_kernel,
        out_shape=[jax.ShapeDtypeStruct((SENT, KV), BF)] * 4,
        in_specs=[VMEM] * 6,
        out_specs=[VMEM] * 4,
        compiler_params=PARAMS,
        name="pack_kv",
    )(k, v, k_in, v_in, sel, sel_in))


def pack_kernel(own, come, sel, sel_in, o0, o1, o2, o3, held, sems):
    core = own_head(0)[1]
    outs, copies = (o0, o1, o2, o3), []
    for step in range(4):
        here = pl.ds(pl.multiple_of(own_head(step)[0] * HALF, HALF), HALF)
        for i, ref in enumerate((own, come)):
            copies.append(pltpu.make_async_copy(ref.at[:, here], held.at[step, i], sems.at[2 * step + i]))
            copies[-1].start()
    pick = compact(jnp.where(core == 1, sel_in[...], sel[...]))
    for step, out in enumerate(outs):
        copies[2 * step].wait()
        copies[2 * step + 1].wait()

        @pl.when(core == 1)
        def _(step=step, out=out):
            out[:ROWS, :] = held[step, 0]
            out[ROWS:, :] = dot(pick, held[step, 1]).astype(BF)

        @pl.when(core == 0)
        def _(step=step, out=out):
            out[:ROWS, :] = held[step, 1]
            out[ROWS:, :] = dot(pick, held[step, 0]).astype(BF)


def pack(own, come, sel, sel_in):
    return list(pl.pallas_call(
        pack_kernel,
        out_shape=[jax.ShapeDtypeStruct((SENT, HALF), BF)] * 4,
        in_specs=[ANY] * 2 + [VMEM] * 2,
        out_specs=[VMEM] * 4,
        scratch_shapes=[pltpu.VMEM((4, 2, ROWS, HALF), BF), pltpu.SemaphoreType.DMA((8,))],
        compiler_params=WHOLE,
        name="pack",
    )(own, come, sel, sel_in))


FORTH = pltpu.CompilerParams(vmem_limit_bytes=12 << 20)
BACK = pltpu.CompilerParams(vmem_limit_bytes=24 << 20)
SUMS = [((DENSE, HEAD), F32)] * 2 + [((FEW, HEAD), F32)] * 2
FEWER = SLOTS * GROUP
LEFT = [((SENT, HALF), BF), ((DENSE, HALF), BF), ((8, HALF), F32), ((HEAD, HALF), F32),
        ((FEW, FEWER), BF), ((8, FEWER), F32), ((HEAD, FEWER), F32)]
KEYS = [((DENSE, HEAD), BF), ((DENSE // CHUNK, HEAD, CHUNK), BF), ((FEW, HEAD), BF), ((FEW // CHUNK, HEAD, CHUNK), BF)]
KEYED = KEYS + KEYS + [((FEW, HEAD), F32)]


def shaped(shapes):
    return [jax.ShapeDtypeStruct(s, d) for s, d in shapes]


def held(shapes):
    return [pltpu.VMEM(s, d) for s, d in shapes]


FORWARD = held([((HALF, HEAD), BF), ((HEAD, HALF), BF), ((DENSE, HALF), F32), ((8, HALF), F32), ((8, HALF), F32)])
BACKWARD = held([((HALF, HEAD), BF), ((HALF, HEAD), BF), ((HEAD, HALF), BF), ((HEAD, HALF), F32), ((8, HALF), F32)])


def cost(flops):
    return pl.CostEstimate(flops=int(flops), bytes_accessed=4 << 20, transcendentals=0)


def turn_blocks(x, xt):
    for c in range(xt.shape[0]):
        xt[c] = x[c * CHUNK:(c + 1) * CHUNK, :].T


def arrange(info, kvs, keyed):
    kd, ktd, kr, ktr, vd, vtd, vr, vtr, flags = keyed
    for ky, kv in enumerate(kvs):
        for kz in range(4):
            b = 4 * lax.rem(info[1] + 4 - kz, 4) + lax.rem(info[2] + 4 - ky, 4)
            big = pl.ds(pl.multiple_of(b * ROWS, ROWS), ROWS)
            small = pl.ds(pl.multiple_of(b * SLOTS, SLOTS), SLOTS)
            kd[big, :] = kv[kz, :ROWS, :HEAD]
            vd[big, :] = kv[kz, :ROWS, HEAD:]
            kr[small, :] = kv[kz, ROWS:, :HEAD]
            vr[small, :] = kv[kz, ROWS:, HEAD:]
            flags[small, :] = (kv[kz, ROWS:, :HEAD].astype(F32) < INVALID / 2).astype(F32)
    for x, xt in ((kd, ktd), (kr, ktr), (vd, vtd), (vr, vtr)):
        turn_blocks(x, xt)


def reach(info, shift):
    blk = 4 * lax.rem(info[1] + 4 - shift, 4) + info[2]
    per = CHUNK // ROWS
    return blk, lax.div(blk + per, per)


def forward_block(info, shift, q, keyed, left, scr):
    kd, _, kr, _, _, vtd, _, vtr, flags = keyed
    attn, e_dense, inv_dense, t_dense, e_few, inv_few, t_few = left
    blk, chunks = reach(info, shift)

    def place(cols):
        shape = (CHUNK, cols)
        return lax.broadcasted_iota(jnp.int32, shape, 0), lax.broadcasted_iota(jnp.int32, shape, 1)

    def causal(c):
        row, col = place(TILE)
        return c * CHUNK + row <= blk * ROWS + lax.rem(col, ROWS)

    def routed(c):
        row, col = place(FEWER)
        near = c * CHUNK + row <= blk * SLOTS + lax.rem(col, SLOTS)
        return near & (jnp.concatenate([flags[at(c), :]] * (FEWER // HEAD), axis=1) > 0.5)

    forward_pass(q[:ROWS, :], ROWS, kd, vtd, e_dense, inv_dense, t_dense, chunks, chunks - 1, causal, scr)
    emit(t_dense, ROWS, 1.0, attn, 0, 0)
    forward_pass(q[ROWS:, :], SLOTS, kr, vtr, e_few, inv_few, t_few, FEW // CHUNK, 0, routed, scr)
    emit(t_few, SLOTS, 1.0, attn, ROWS, 0)


def forward_kernel(shifts, first, info, *refs):
    n, m = len(shifts), len(LEFT)
    qs, refs = refs[:n], refs[n:]
    if first:
        kvs, refs = refs[:4], refs[4:]
    else:
        keyed, refs = refs[:9], refs[9:]
    lefts, refs = refs[:m * n], refs[m * n:]
    if first:
        keyed, refs = refs[:9], refs[9:]
        arrange(info, kvs, keyed)
    for i, shift in enumerate(shifts):
        forward_block(info, shift, qs[i], keyed, lefts[m * i:m * (i + 1)], refs)


def forward(shifts, info, qs, kvs=None, keyed=None):
    n, m, first = len(shifts), len(LEFT), kvs is not None
    shapes = LEFT * n + (KEYED if first else [])
    others = list(kvs if first else keyed)
    outs = pl.pallas_call(
        functools.partial(forward_kernel, shifts, first),
        out_shape=shaped(shapes),
        in_specs=[SMEM] + [VMEM] * (n + len(others)),
        out_specs=[VMEM] * len(shapes),
        scratch_shapes=FORWARD,
        compiler_params=FORTH,
        cost_estimate=cost(n * 4e9),
        name="forward",
    )(info, *qs, *others)
    lefts = [list(outs[m * i:m * (i + 1)]) for i in range(n)]
    return (lefts, outs[m * n:]) if first else lefts


def backward_block(info, shift, q, g, keyed, left, sums, dq, scr):
    _, ktd, _, ktr, vd, _, vr, _, _ = keyed
    _, chunks = reach(info, shift)
    backward_pass(q[:ROWS, :], g[:ROWS, :], ROWS, vd, ktd, *left[:3], *sums[:2], chunks, scr)
    emit(scr[3], ROWS, SCALE, dq, 0, 0)
    backward_pass(q[ROWS:, :], g[ROWS:, :], SLOTS, vr, ktr, *left[3:], *sums[2:], FEW // CHUNK, scr)
    emit(scr[3], SLOTS, SCALE, dq, ROWS, 0)


def backward_kernel(shifts, info, *refs):
    n, m = len(shifts), len(LEFT) - 1
    qs, gs, refs = refs[:n], refs[n:2 * n], refs[2 * n:]
    lefts, keyed, refs = refs[:m * n], refs[m * n:m * n + 9], refs[m * n + 9:]
    dqs, sent, sums, scr = refs[:n], refs[n:n + 4], refs[n + 4:n + 8], refs[n + 8:]
    for total in sums:
        total[...] = jnp.zeros_like(total)
    for i, shift in enumerate(shifts):
        backward_block(info, shift, qs[i], gs[i], keyed, lefts[m * i:m * (i + 1)], sums, dqs[i], scr)
    for ky in range(4):
        for kz in range(4):
            b = 4 * lax.rem(info[1] + kz, 4) + lax.rem(info[2] + ky, 4)
            big = pl.ds(pl.multiple_of(b * ROWS, ROWS), ROWS)
            small = pl.ds(pl.multiple_of(b * SLOTS, SLOTS), SLOTS)
            sent[ky][kz, :ROWS, :HEAD] = (sums[0][big, :] * SCALE).astype(BF)
            sent[ky][kz, :ROWS, HEAD:] = sums[1][big, :].astype(BF)
            sent[ky][kz, ROWS:, :HEAD] = (sums[2][small, :] * SCALE).astype(BF)
            sent[ky][kz, ROWS:, HEAD:] = sums[3][small, :].astype(BF)


def backward(shifts, info, qs, gs, lefts, keyed):
    n = len(shifts)
    shapes = [((SENT, HALF), BF)] * n + [((4, SENT, KV), BF)] * 4
    args = [qs[i] for i in shifts] + [gs[i] for i in shifts] + [x for i in shifts for x in lefts[i][1:]] + list(keyed)
    outs = pl.pallas_call(
        functools.partial(backward_kernel, shifts),
        out_shape=shaped(shapes),
        in_specs=[SMEM] + [VMEM] * len(args),
        out_specs=[VMEM] * len(shapes),
        scratch_shapes=held(SUMS) + BACKWARD,
        compiler_params=BACK,
        cost_estimate=cost(n * 6e9),
        name="backward",
    )(info, *args)
    return list(outs[:n]), list(outs[n:])


def fold_kernel(a, b, c, d, *outs):
    for i, out in enumerate(outs):
        total = a[i].astype(F32) + b[i].astype(F32) + c[i].astype(F32) + d[i].astype(F32)
        out[...] = total.astype(BF)


def fold_sums(parts):
    return list(pl.pallas_call(
        fold_kernel,
        out_shape=[jax.ShapeDtypeStruct((SENT, KV), BF)] * 4,
        in_specs=[VMEM] * 4,
        out_specs=[VMEM] * 4,
        compiler_params=PARAMS,
        name="fold_sums",
    )(*parts))


def heads_of(info, sel, mine, theirs, put):
    @pl.when(info[0] == 1)
    def _():
        put(0, theirs[0, :ROWS, :].astype(F32))
        put(1, mine[0, :ROWS, :].astype(F32))

    @pl.when(info[0] == 0)
    def _():
        pick = chooser(sel)[:, :SLOTS].astype(BF)
        put(0, dot(pick, mine[0, ROWS:, :]))
        put(1, dot(pick, theirs[0, ROWS:, :]))


def update_kernel(info, seg, mine, theirs, sel, out):
    def put(i, x):
        cols = slice(i * HALF, (i + 1) * HALF)
        out[:, cols] = (seg[:, cols].astype(F32) + x).astype(BF)

    heads_of(info, sel, mine, theirs, put)


def finish_q_kernel(info, mine, theirs, sel, out):
    def put(i, x):
        out[:, i * HALF:(i + 1) * HALF] = x.astype(BF)

    heads_of(info, sel, mine, theirs, put)


def by_head(kernel, name, info, seg, mine, theirs, sel):
    part = pl.BlockSpec((1, SENT, HALF), lambda i, info: (i, 0, 0))
    whole = pl.BlockSpec((ROWS, 2 * HALF), lambda i, info: (0, lax.rem(info[1] + i, 4)))
    segs = [] if seg is None else [seg]
    return pl.pallas_call(
        kernel,
        grid_spec=pltpu.PrefetchScalarGridSpec(
            num_scalar_prefetch=1,
            grid=(4,),
            in_specs=[whole] * len(segs) + [part, part, SEL],
            out_specs=whole,
        ),
        out_shape=jax.ShapeDtypeStruct((ROWS, 8 * HALF), BF),
        compiler_params=PARAMS,
        name=name,
    )(info, *segs, mine, theirs, sel)


def settle_kernel(x, out):
    out[...] = x[...]


def settle(x):
    part = pl.BlockSpec((ROWS, 2 * HALF), lambda i: (0, i))
    return pl.pallas_call(
        settle_kernel,
        grid=(4,),
        in_specs=[part],
        out_specs=part,
        out_shape=jax.ShapeDtypeStruct(x.shape, x.dtype),
        compiler_params=PARAMS,
        name="settle",
    )(x)


def finish_kv_kernel(info, sums, sums_in, sel, dk, dv):
    def fill(even, odd, rows):
        for shift in range(4):
            for i, ref in enumerate((even, odd)):
                head = 2 * lax.rem(info[1] + 4 - shift, 4) + i
                at = pl.ds(pl.multiple_of(head * HEAD, HEAD), HEAD)
                x = rows(ref[shift])
                dk[:, at] = x[:, :HEAD]
                dv[:, at] = x[:, HEAD:]

    @pl.when(info[0] == 1)
    def _():
        fill(sums_in, sums, lambda x: x[:ROWS, :])

    @pl.when(info[0] == 0)
    def _():
        pick = chooser(sel)[:, :SLOTS].astype(BF)
        fill(sums, sums_in, lambda x: dot(pick, x[ROWS:, :]).astype(BF))


def finish_kv(info, sums, sums_in, sel):
    return pl.pallas_call(
        finish_kv_kernel,
        out_shape=[jax.ShapeDtypeStruct((ROWS, 8 * HEAD), BF)] * 2,
        in_specs=[SMEM] + [VMEM] * 3,
        out_specs=[VMEM] * 2,
        compiler_params=PARAMS,
        name="finish_kv",
    )(info, sums, sums_in, sel)


def along_z(x, by):
    return lax.ppermute(x, "ctx", [(4 * z + y, 4 * ((z + by) % 4) + y) for z in range(4) for y in range(4)])


def along_y(x, by):
    return lax.ppermute(x, "ctx", [(4 * z + y, 4 * z + (y + by) % 4) for z in range(4) for y in range(4)])


def swap(x):
    return lax.ppermute(x, "section", [(i, i ^ 1) for i in range(8)])


def onward(x):
    return lax.ppermute(x, "section", [(i, i + 1) for i in range(7)])


def both(*xs):
    return lax.optimization_barrier(xs)


def body(segment_input, queries, keys, values, cotangent, selected, counts):
    section, place = lax.axis_index("section"), lax.axis_index("ctx")
    info = jnp.stack([section % 2, place // 4, place % 4]).astype(jnp.int32)
    seg, q, k, v, g = (x[0] for x in (segment_input, queries, keys, values, cotangent))
    sel = jnp.where(jnp.arange(ROWS, dtype=jnp.int32)[None, :] < counts, selected, -1)

    k_in, v_in, sel_in = swap(k), swap(v), swap(sel)
    kv = pack_kv(k, v, k_in, v_in, sel, sel_in)
    q, g, *_ = both(q, g, k_in, v_in, sel_in)
    q_in, g_in = swap(q), swap(g)
    qs = pack(q, q_in, sel, sel_in)
    for by in (1, 3, 2):
        kv[by] = along_z(kv[by], by)
    kv[1], kv[2], kv[3], qs[1], qs[2], qs[3], g_in = both(kv[1], kv[2], kv[3], qs[1], qs[2], qs[3], g_in)
    column = jnp.stack(kv)
    kvs = [column] + [along_y(column, by) for by in (1, 2, 3)]
    qs[1], qs[2], qs[3], g_in, _ = both(qs[1], qs[2], qs[3], g_in, column)
    for by in (1, 3, 2):
        qs[by] = along_z(qs[by], by)
    gs = pack(g, g_in, sel, sel_in)

    qs[0], qs[1], qs[3] = both(qs[0], qs[1], qs[3])
    (own,), keyed = forward((0,), info, [qs[0]], kvs=kvs)
    for by in (1, 3, 2):
        gs[by] = along_z(gs[by], by)
    one, three, two = forward((1, 3, 2), info, [qs[1], qs[3], qs[2]], keyed=keyed)
    lefts = [own, one, two, three]
    attn = [along_z(lefts[by][0], 4 - by) if by else lefts[by][0] for by in range(4)]
    dq, sent = backward((1, 3, 0, 2), info, qs, gs, lefts, keyed)
    dq = [dq[2], dq[0], dq[3], dq[1]]
    dq = [along_z(dq[by], 4 - by) if by else dq[by] for by in range(4)]
    attn[1], attn[2], attn[3], sent[0] = both(attn[1], attn[2], attn[3], sent[0])
    dq[1], dq[3], sent[1] = both(dq[1], dq[3], sent[1])
    attn = jnp.stack(attn)
    updated = by_head(update_kernel, "update", info, seg, attn, swap(attn), sel)
    next_input = onward(updated)
    sums = fold_sums([sent[0]] + [along_y(sent[by], by) for by in (1, 2, 3)])
    dq[2], sums[0] = both(dq[2], sums[0])
    dq = jnp.stack(dq)
    query_grad = by_head(finish_q_kernel, "finish_q", info, None, dq, swap(dq), sel)
    sums = [sums[0]] + [along_z(sums[by], by) for by in (1, 2, 3)]
    next_input, query_grad, *sums = both(settle(next_input), query_grad, *sums)
    sums = jnp.stack(sums)
    key_grad, value_grad = finish_kv(info, sums, swap(sums), sel)
    return next_input[None], query_grad[None], key_grad[None], value_grad[None]


def solution(mesh):
    wide, thin = P("section", "ctx", None), P("section", "ctx")
    return jax.shard_map(
        body,
        mesh=mesh,
        in_specs=(wide,) * 5 + (thin,) * 2,
        out_specs=(wide,) * 4,
        check_vma=False,
    )
```

```python
import functools, math
import jax, jax.numpy as jnp
from jax import lax
from jax.experimental import pallas as pl
from jax.experimental.pallas import tpu as pltpu
from jax.sharding import PartitionSpec as P

HEAD = 128
GROUP = 8
ROWS = 128
SLOTS = 32
BLOCKS = 16
CHUNK = 512
TILE = 512
SCALE = HEAD ** -0.5
LOG2E = math.log2(math.e)
BF = jnp.bfloat16
F32 = jnp.float32


def dot(a, b):
    return jnp.dot(a, b, preferred_element_type=F32)


def fold(x, op):
    return op(x.reshape(x.shape[0] // 8, 8, x.shape[1]), axis=0)


def turned(x, width, rows, out):
    cols = width * GROUP
    for h in range(GROUP):
        rows[h * width:(h + 1) * width, :] = x[:, h * HEAD:(h + 1) * HEAD]
    for t in range(0, cols, HEAD):
        out[:, t:t + HEAD] = rows[t:t + HEAD, :].T


def tiles_of(cols, tile):
    tile = min(tile, cols)
    return [slice(t, t + tile) for t in range(0, cols, tile)]


def at(c):
    return pl.ds(pl.multiple_of(c * CHUNK, CHUNK), CHUNK)


def loop(first, end, fn):
    lax.fori_loop(first, end, lambda c, z: (fn(c), z)[1], 0)


def forward_pass(q, width, k_ref, vt_ref, e_ref, stat, acc, chunks, full, mask_of, scr):
    rows, qt, s_scr, m_scr, l_scr = scr
    cols = width * GROUP
    turned(q, width, rows, qt)
    tiles = tiles_of(cols, TILE)
    m_scr[:, :cols] = jnp.full((8, cols), -1e30, F32)
    l_scr[:, :cols] = jnp.zeros((8, cols), F32)
    acc[...] = jnp.zeros((HEAD, cols), F32)

    def score(c, masked):
        k = k_ref[at(c), :]
        for t in tiles:
            s = dot(k, qt[:, t])
            if masked:
                s = jnp.where(mask_of(c), s, -1e30)
            s_scr[at(c), t] = s
            m_scr[:, t] = jnp.maximum(m_scr[:, t], fold(s, jnp.max))

    loop(0, full, lambda c: score(c, False))
    loop(full, chunks, lambda c: score(c, True))
    top = jnp.max(m_scr[:, :cols], axis=0, keepdims=True) * (SCALE * LOG2E)
    m_scr[:, :cols] = jnp.broadcast_to(top, (8, cols))

    def weigh(c):
        for t in tiles:
            e = jnp.exp2(s_scr[at(c), t] * (SCALE * LOG2E) - m_scr[0:1, t])
            l_scr[:, t] += fold(e, jnp.sum)
            eb = e.astype(BF)
            e_ref[at(c), t] = eb
            acc[:, t] += dot(vt_ref[c], eb)

    loop(0, chunks, weigh)
    inv = 1.0 / jnp.sum(l_scr[:, :cols], axis=0, keepdims=True)
    acc[:, :cols] = acc[:, :cols] * inv
    stat[...] = jnp.broadcast_to(inv, (8, cols))


def backward_pass(q, g, width, v_ref, kt_ref, e_ref, stat, attn_t, dk_ref, dv_ref, chunks, scr):
    qs, gs, gt, acc, d_scr = scr
    cols = width * GROUP
    for h in range(GROUP):
        qs[h * width:(h + 1) * width, :] = q[:, h * HEAD:(h + 1) * HEAD]
    turned(g, width, gs, gt)
    for t in range(0, cols, HEAD):
        part = (gt[:, t:t + HEAD].astype(F32) * stat[0:1, t:t + HEAD]).astype(BF)
        gt[:, t:t + HEAD] = part
        gs[t:t + HEAD, :] = part.T
    tiles = tiles_of(cols, HALF)
    acc[:, :cols] = jnp.zeros((HEAD, cols), F32)
    delta = jnp.sum(attn_t[...] * gt[:, :cols].astype(F32), axis=0, keepdims=True)
    d_scr[:, :cols] = jnp.broadcast_to(delta, (8, cols))

    def back(c):
        v = v_ref[at(c), :]
        dk = dk_ref[at(c), :]
        dv = dv_ref[at(c), :]
        for t in tiles:
            e = e_ref[at(c), t]
            ds = (e.astype(F32) * (dot(v, gt[:, t]) - d_scr[0:1, t])).astype(BF)
            dv += dot(e, gs[t, :])
            dk += dot(ds, qs[t, :])
            acc[:, t] += dot(kt_ref[c], ds)
        dk_ref[at(c), :] = dk
        dv_ref[at(c), :] = dv

    loop(0, chunks, back)


def emit(src, width, scale, out, row, col):
    for t in range(width * GROUP // 128):
        x = (src[:, t * 128:(t + 1) * 128] * scale).T.astype(BF)
        per = 128 // width
        for i in range(per):
            h = t * per + i
            out[row:row + width, col + h * HEAD:col + (h + 1) * HEAD] = x[i * width:(i + 1) * width, :]


def chooser(sel):
    return (lax.broadcasted_iota(jnp.int32, (ROWS, ROWS), 0) == sel[0:1, :]).astype(F32)


def compact(sel):
    return chooser(sel).T[:SLOTS, :].astype(BF)


HALF = GROUP * HEAD
QG = 2 * HALF
KV = 2 * HEAD
DENSE = BLOCKS * ROWS
FEW = BLOCKS * SLOTS
SENT = ROWS + SLOTS
INVALID = 128.0
VMEM = pl.BlockSpec(memory_space=pltpu.VMEM)
SMEM = pl.BlockSpec(memory_space=pltpu.SMEM)
WHOLE = pltpu.CompilerParams(vmem_limit_bytes=60 << 20)
PARAMS = pltpu.CompilerParams(vmem_limit_bytes=16 << 20)
ANY = pl.BlockSpec(memory_space=pl.ANY)
SEL = pl.BlockSpec((1, ROWS), lambda i, info: (0, 0))


def own_head(shift):
    core, z = lax.rem(lax.axis_index("section"), 2), lax.div(lax.axis_index("ctx"), 4)
    return 2 * lax.rem(z + shift, 4) + core, core


def pack_kv_kernel(own, come, sel, sel_in, *outs):
    def fill(dense, few, few_sel):
        pick = compact(few_sel)
        mark = INVALID * (1.0 - jnp.sum(pick.astype(F32), axis=1, keepdims=True))
        for step, out in enumerate(outs):
            for side in range(2):
                here = pl.ds(pl.multiple_of(own_head(step)[0] * HEAD + side * HALF, HEAD), HEAD)
                cols = slice(side * HEAD, (side + 1) * HEAD)
                out[:ROWS, cols] = dense[:, here]
                rows = dot(pick, few[:, here])
                out[ROWS:, cols] = (rows if side else rows + mark).astype(BF)

    @pl.when(own_head(0)[1] == 1)
    def _():
        fill(own, come, sel_in)

    @pl.when(own_head(0)[1] == 0)
    def _():
        fill(come, own, sel)


def pack_kv(own, come, sel, sel_in):
    return list(pl.pallas_call(
        pack_kv_kernel,
        out_shape=[jax.ShapeDtypeStruct((SENT, KV), BF)] * 4,
        in_specs=[VMEM] * 4,
        out_specs=[VMEM] * 4,
        compiler_params=PARAMS,
        name="pack_kv",
    )(own, come, sel, sel_in))


def pack_kernel(own, come, sel, sel_in, o0, o1, o2, o3, held, sems):
    core = own_head(0)[1]
    outs, copies = (o0, o1, o2, o3), []
    for step in range(4):
        here = pl.ds(pl.multiple_of(own_head(step)[0] * HALF, HALF), HALF)
        for i, ref in enumerate((own, come)):
            copies.append(pltpu.make_async_copy(ref.at[:, here], held.at[step, i], sems.at[2 * step + i]))
            copies[-1].start()
    pick = compact(jnp.where(core == 1, sel_in[...], sel[...]))
    for step, out in enumerate(outs):
        copies[2 * step].wait()
        copies[2 * step + 1].wait()

        @pl.when(core == 1)
        def _(step=step, out=out):
            out[:ROWS, :] = held[step, 0]
            out[ROWS:, :] = dot(pick, held[step, 1]).astype(BF)

        @pl.when(core == 0)
        def _(step=step, out=out):
            out[:ROWS, :] = held[step, 1]
            out[ROWS:, :] = dot(pick, held[step, 0]).astype(BF)


def pack(own, come, sel, sel_in, params):
    return list(pl.pallas_call(
        pack_kernel,
        out_shape=[jax.ShapeDtypeStruct((SENT, HALF), BF)] * 4,
        in_specs=[ANY] * 2 + [VMEM] * 2,
        out_specs=[VMEM] * 4,
        scratch_shapes=[pltpu.VMEM((4, 2, ROWS, HALF), BF), pltpu.SemaphoreType.DMA((8,))],
        compiler_params=params,
        name="pack",
    )(own, come, sel, sel_in))


FORTH = pltpu.CompilerParams(vmem_limit_bytes=12 << 20)
BACK = pltpu.CompilerParams(vmem_limit_bytes=24 << 20)
SUMS = [((DENSE, HEAD), F32)] * 2 + [((FEW, HEAD), F32)] * 2
FEWER = SLOTS * GROUP
LEFT = [((SENT, HALF), BF), ((DENSE, HALF), BF), ((8, HALF), F32), ((HEAD, HALF), F32),
        ((FEW, FEWER), BF), ((8, FEWER), F32), ((HEAD, FEWER), F32)]
KEYS = [((DENSE, HEAD), BF), ((DENSE // CHUNK, HEAD, CHUNK), BF), ((FEW, HEAD), BF), ((FEW // CHUNK, HEAD, CHUNK), BF)]
KEYED = KEYS + KEYS + [((FEW, HEAD), F32)]


def shaped(shapes):
    return [jax.ShapeDtypeStruct(s, d) for s, d in shapes]


def held(shapes):
    return [pltpu.VMEM(s, d) for s, d in shapes]


FORWARD = held([((HALF, HEAD), BF), ((HEAD, HALF), BF), ((DENSE, HALF), F32), ((8, HALF), F32), ((8, HALF), F32)])
BACKWARD = held([((HALF, HEAD), BF), ((HALF, HEAD), BF), ((HEAD, HALF), BF), ((HEAD, HALF), F32), ((8, HALF), F32)])


def cost(flops):
    return pl.CostEstimate(flops=int(flops), bytes_accessed=4 << 20, transcendentals=0)


def turn_blocks(x, xt):
    for c in range(xt.shape[0]):
        xt[c] = x[c * CHUNK:(c + 1) * CHUNK, :].T


def arrange(info, kvs, keyed):
    kd, ktd, kr, ktr, vd, vtd, vr, vtr, flags = keyed
    for ky, kv in enumerate(kvs):
        for kz in range(4):
            b = 4 * lax.rem(info[1] + 4 - kz, 4) + lax.rem(info[2] + 4 - ky, 4)
            big = pl.ds(pl.multiple_of(b * ROWS, ROWS), ROWS)
            small = pl.ds(pl.multiple_of(b * SLOTS, SLOTS), SLOTS)
            kd[big, :] = kv[kz, :ROWS, :HEAD]
            vd[big, :] = kv[kz, :ROWS, HEAD:]
            kr[small, :] = kv[kz, ROWS:, :HEAD]
            vr[small, :] = kv[kz, ROWS:, HEAD:]
            flags[small, :] = (kv[kz, ROWS:, :HEAD].astype(F32) < INVALID / 2).astype(F32)
    for x, xt in ((kd, ktd), (kr, ktr), (vd, vtd), (vr, vtr)):
        turn_blocks(x, xt)


def reach(info, shift):
    blk = 4 * lax.rem(info[1] + 4 - shift, 4) + info[2]
    per = CHUNK // ROWS
    return blk, lax.div(blk + per, per)


def forward_block(info, shift, q, keyed, left, scr):
    kd, _, kr, _, _, vtd, _, vtr, flags = keyed
    attn, e_dense, inv_dense, t_dense, e_few, inv_few, t_few = left
    blk, chunks = reach(info, shift)

    def place(cols):
        shape = (CHUNK, cols)
        return lax.broadcasted_iota(jnp.int32, shape, 0), lax.broadcasted_iota(jnp.int32, shape, 1)

    def causal(c):
        row, col = place(TILE)
        return c * CHUNK + row <= blk * ROWS + lax.rem(col, ROWS)

    def routed(c):
        row, col = place(FEWER)
        near = c * CHUNK + row <= blk * SLOTS + lax.rem(col, SLOTS)
        return near & (jnp.concatenate([flags[at(c), :]] * (FEWER // HEAD), axis=1) > 0.5)

    forward_pass(q[:ROWS, :], ROWS, kd, vtd, e_dense, inv_dense, t_dense, chunks, chunks - 1, causal, scr)
    emit(t_dense, ROWS, 1.0, attn, 0, 0)
    forward_pass(q[ROWS:, :], SLOTS, kr, vtr, e_few, inv_few, t_few, FEW // CHUNK, 0, routed, scr)
    emit(t_few, SLOTS, 1.0, attn, ROWS, 0)


def forward_kernel(shifts, first, info, *refs):
    n, m = len(shifts), len(LEFT)
    qs, refs = refs[:n], refs[n:]
    if first:
        kvs, refs = refs[:4], refs[4:]
    else:
        keyed, refs = refs[:9], refs[9:]
    lefts, refs = refs[:m * n], refs[m * n:]
    if first:
        keyed, refs = refs[:9], refs[9:]
        arrange(info, kvs, keyed)
    for i, shift in enumerate(shifts):
        forward_block(info, shift, qs[i], keyed, lefts[m * i:m * (i + 1)], refs)


def forward(shifts, info, qs, kvs=None, keyed=None):
    n, m, first = len(shifts), len(LEFT), kvs is not None
    shapes = LEFT * n + (KEYED if first else [])
    others = list(kvs if first else keyed)
    outs = pl.pallas_call(
        functools.partial(forward_kernel, shifts, first),
        out_shape=shaped(shapes),
        in_specs=[SMEM] + [VMEM] * (n + len(others)),
        out_specs=[VMEM] * len(shapes),
        scratch_shapes=FORWARD,
        compiler_params=FORTH,
        cost_estimate=cost(n * 4e9),
        name="forward",
    )(info, *qs, *others)
    lefts = [list(outs[m * i:m * (i + 1)]) for i in range(n)]
    return (lefts, outs[m * n:]) if first else lefts


def backward_block(info, shift, q, g, keyed, left, sums, dq, scr):
    _, ktd, _, ktr, vd, _, vr, _, _ = keyed
    _, chunks = reach(info, shift)
    backward_pass(q[:ROWS, :], g[:ROWS, :], ROWS, vd, ktd, *left[:3], *sums[:2], chunks, scr)
    emit(scr[3], ROWS, SCALE, dq, 0, 0)
    backward_pass(q[ROWS:, :], g[ROWS:, :], SLOTS, vr, ktr, *left[3:], *sums[2:], FEW // CHUNK, scr)
    emit(scr[3], SLOTS, SCALE, dq, ROWS, 0)


def backward_kernel(shifts, info, *refs):
    n, m = len(shifts), len(LEFT) - 1
    qs, gs, refs = refs[:n], refs[n:2 * n], refs[2 * n:]
    lefts, keyed, refs = refs[:m * n], refs[m * n:m * n + 9], refs[m * n + 9:]
    dqs, sent, sums, scr = refs[:n], refs[n:n + 4], refs[n + 4:n + 8], refs[n + 8:]
    for total in sums:
        total[...] = jnp.zeros_like(total)
    for i, shift in enumerate(shifts):
        backward_block(info, shift, qs[i], gs[i], keyed, lefts[m * i:m * (i + 1)], sums, dqs[i], scr)
    for ky in range(4):
        for kz in range(4):
            b = 4 * lax.rem(info[1] + kz, 4) + lax.rem(info[2] + ky, 4)
            big = pl.ds(pl.multiple_of(b * ROWS, ROWS), ROWS)
            small = pl.ds(pl.multiple_of(b * SLOTS, SLOTS), SLOTS)
            sent[ky][kz, :ROWS, :HEAD] = (sums[0][big, :] * SCALE).astype(BF)
            sent[ky][kz, :ROWS, HEAD:] = sums[1][big, :].astype(BF)
            sent[ky][kz, ROWS:, :HEAD] = (sums[2][small, :] * SCALE).astype(BF)
            sent[ky][kz, ROWS:, HEAD:] = sums[3][small, :].astype(BF)


def backward(shifts, info, qs, gs, lefts, keyed):
    n = len(shifts)
    shapes = [((SENT, HALF), BF)] * n + [((4, SENT, KV), BF)] * 4
    args = [qs[i] for i in shifts] + [gs[i] for i in shifts] + [x for i in shifts for x in lefts[i][1:]] + list(keyed)
    outs = pl.pallas_call(
        functools.partial(backward_kernel, shifts),
        out_shape=shaped(shapes),
        in_specs=[SMEM] + [VMEM] * len(args),
        out_specs=[VMEM] * len(shapes),
        scratch_shapes=held(SUMS) + BACKWARD,
        compiler_params=BACK,
        cost_estimate=cost(n * 6e9),
        name="backward",
    )(info, *args)
    return list(outs[:n]), list(outs[n:])


def fold_kernel(a, b, c, d, *outs):
    for i, out in enumerate(outs):
        total = a[i].astype(F32) + b[i].astype(F32) + c[i].astype(F32) + d[i].astype(F32)
        out[...] = total.astype(BF)


def fold_sums(parts):
    return list(pl.pallas_call(
        fold_kernel,
        out_shape=[jax.ShapeDtypeStruct((SENT, KV), BF)] * 4,
        in_specs=[VMEM] * 4,
        out_specs=[VMEM] * 4,
        compiler_params=PARAMS,
        name="fold_sums",
    )(*parts))


def heads_of(info, sel, mine, theirs, put):
    @pl.when(info[0] == 1)
    def _():
        put(0, theirs[0, :ROWS, :].astype(F32))
        put(1, mine[0, :ROWS, :].astype(F32))

    @pl.when(info[0] == 0)
    def _():
        pick = chooser(sel)[:, :SLOTS].astype(BF)
        put(0, dot(pick, mine[0, ROWS:, :]))
        put(1, dot(pick, theirs[0, ROWS:, :]))


def update_kernel(info, seg, mine, theirs, sel, out):
    def put(i, x):
        cols = slice(i * HALF, (i + 1) * HALF)
        out[:, cols] = (seg[:, cols].astype(F32) + x).astype(BF)

    heads_of(info, sel, mine, theirs, put)


def finish_q_kernel(info, mine, theirs, sel, out):
    def put(i, x):
        out[:, i * HALF:(i + 1) * HALF] = x.astype(BF)

    heads_of(info, sel, mine, theirs, put)


def by_head(kernel, name, info, seg, mine, theirs, sel):
    part = pl.BlockSpec((1, SENT, HALF), lambda i, info: (i, 0, 0))
    whole = pl.BlockSpec((ROWS, 2 * HALF), lambda i, info: (0, lax.rem(info[1] + i, 4)))
    segs = [] if seg is None else [seg]
    return pl.pallas_call(
        kernel,
        grid_spec=pltpu.PrefetchScalarGridSpec(
            num_scalar_prefetch=1,
            grid=(4,),
            in_specs=[whole] * len(segs) + [part, part, SEL],
            out_specs=whole,
        ),
        out_shape=jax.ShapeDtypeStruct((ROWS, 8 * HALF), BF),
        compiler_params=PARAMS,
        name=name,
    )(info, *segs, mine, theirs, sel)


def settle_kernel(x, out):
    out[...] = x[...]


def settle(x):
    part = pl.BlockSpec((ROWS, 2 * HALF), lambda i: (0, i))
    return pl.pallas_call(
        settle_kernel,
        grid=(4,),
        in_specs=[part],
        out_specs=part,
        out_shape=jax.ShapeDtypeStruct(x.shape, x.dtype),
        compiler_params=PARAMS,
        name="settle",
    )(x)


def finish_kv_kernel(info, sums, sums_in, sel, dk, dv):
    def fill(even, odd, rows):
        for shift in range(4):
            for i, ref in enumerate((even, odd)):
                head = 2 * lax.rem(info[1] + 4 - shift, 4) + i
                at = pl.ds(pl.multiple_of(head * HEAD, HEAD), HEAD)
                x = rows(ref[shift])
                dk[:, at] = x[:, :HEAD]
                dv[:, at] = x[:, HEAD:]

    @pl.when(info[0] == 1)
    def _():
        fill(sums_in, sums, lambda x: x[:ROWS, :])

    @pl.when(info[0] == 0)
    def _():
        pick = chooser(sel)[:, :SLOTS].astype(BF)
        fill(sums, sums_in, lambda x: dot(pick, x[ROWS:, :]).astype(BF))


def finish_kv(info, sums, sums_in, sel):
    return pl.pallas_call(
        finish_kv_kernel,
        out_shape=[jax.ShapeDtypeStruct((ROWS, 8 * HEAD), BF)] * 2,
        in_specs=[SMEM] + [VMEM] * 3,
        out_specs=[VMEM] * 2,
        compiler_params=PARAMS,
        name="finish_kv",
    )(info, sums, sums_in, sel)


def along_z(x, by):
    return lax.ppermute(x, "ctx", [(4 * z + y, 4 * ((z + by) % 4) + y) for z in range(4) for y in range(4)])


def along_y(x, by):
    return lax.ppermute(x, "ctx", [(4 * z + y, 4 * z + (y + by) % 4) for z in range(4) for y in range(4)])


def swap(x):
    return lax.ppermute(x, "section", [(i, i ^ 1) for i in range(8)])


def onward(x):
    return lax.ppermute(x, "section", [(i, i + 1) for i in range(7)])


def both(*xs):
    return lax.optimization_barrier(xs)


def body(segment_input, queries, keys, values, cotangent, selected, counts):
    section, place = lax.axis_index("section"), lax.axis_index("ctx")
    info = jnp.stack([section % 2, place // 4, place % 4]).astype(jnp.int32)
    seg, q, k, v, g = (x[0] for x in (segment_input, queries, keys, values, cotangent))
    sel = jnp.where(jnp.arange(ROWS, dtype=jnp.int32)[None, :] < counts, selected, -1)

    own = jnp.concatenate([k, v], 1)
    come, sel_in = swap(own), swap(sel)
    kv = pack_kv(own, come, sel, sel_in)
    q, g, *_ = both(q, g, come, sel_in)
    q_in, g_in = swap(q), swap(g)
    qs = pack(q, q_in, sel, sel_in, WHOLE)
    for by in (1, 3, 2):
        kv[by] = along_z(kv[by], by)
    kv[1], kv[2], kv[3], qs[1], qs[2], qs[3], g_in = both(kv[1], kv[2], kv[3], qs[1], qs[2], qs[3], g_in)
    column = jnp.stack(kv)
    kvs = [column] + [along_y(column, by) for by in (1, 2, 3)]
    qs[1], qs[2], qs[3], g_in, _ = both(qs[1], qs[2], qs[3], g_in, column)
    for by in (1, 3, 2):
        qs[by] = along_z(qs[by], by)
    gs = pack(g, g_in, sel, sel_in, PARAMS)

    qs[0], qs[1], qs[3] = both(qs[0], qs[1], qs[3])
    (own,), keyed = forward((0,), info, [qs[0]], kvs=kvs)
    for by in (1, 3, 2):
        gs[by] = along_z(gs[by], by)
    one, three, two = forward((1, 3, 2), info, [qs[1], qs[3], qs[2]], keyed=keyed)
    lefts = [own, one, two, three]
    attn = [along_z(lefts[by][0], 4 - by) if by else lefts[by][0] for by in range(4)]
    dq, sent = backward((1, 3, 0, 2), info, qs, gs, lefts, keyed)
    dq = [dq[2], dq[0], dq[3], dq[1]]
    dq = [along_z(dq[by], 4 - by) if by else dq[by] for by in range(4)]
    attn[1], attn[2], attn[3], sent[0] = both(attn[1], attn[2], attn[3], sent[0])
    dq[1], dq[3], sent[1] = both(dq[1], dq[3], sent[1])
    attn = jnp.stack(attn)
    updated = by_head(update_kernel, "update", info, seg, attn, swap(attn), sel)
    next_input = onward(updated)
    sums = fold_sums([sent[0]] + [along_y(sent[by], by) for by in (1, 2, 3)])
    dq[2], sums[0] = both(dq[2], sums[0])
    dq = jnp.stack(dq)
    query_grad = by_head(finish_q_kernel, "finish_q", info, None, dq, swap(dq), sel)
    sums = [sums[0]] + [along_z(sums[by], by) for by in (1, 2, 3)]
    next_input, query_grad, *sums = both(settle(next_input), query_grad, *sums)
    sums = jnp.stack(sums)
    key_grad, value_grad = finish_kv(info, sums, swap(sums), sel)
    return next_input[None], query_grad[None], key_grad[None], value_grad[None]


def solution(mesh):
    wide, thin = P("section", "ctx", None), P("section", "ctx")
    return jax.shard_map(
        body,
        mesh=mesh,
        in_specs=(wide,) * 5 + (thin,) * 2,
        out_specs=(wide,) * 4,
        check_vma=False,
    )
```

```python
import functools, math
import jax, jax.numpy as jnp
from jax import lax
from jax.experimental import pallas as pl
from jax.experimental.pallas import tpu as pltpu
from jax.sharding import PartitionSpec as P

HEAD = 128
GROUP = 8
ROWS = 128
SLOTS = 32
BLOCKS = 16
CHUNK = 512
TILE = 512
SCALE = HEAD ** -0.5
LOG2E = math.log2(math.e)
BF = jnp.bfloat16
F32 = jnp.float32


def dot(a, b):
    return jnp.dot(a, b, preferred_element_type=F32)


def fold(x, op):
    return op(x.reshape(x.shape[0] // 8, 8, x.shape[1]), axis=0)


def turned(x, width, rows, out):
    cols = width * GROUP
    for h in range(GROUP):
        rows[h * width:(h + 1) * width, :] = x[:, h * HEAD:(h + 1) * HEAD]
    for t in range(0, cols, HEAD):
        out[:, t:t + HEAD] = rows[t:t + HEAD, :].T


def tiles_of(cols, tile):
    tile = min(tile, cols)
    return [slice(t, t + tile) for t in range(0, cols, tile)]


def at(c):
    return pl.ds(pl.multiple_of(c * CHUNK, CHUNK), CHUNK)


def loop(first, end, fn):
    lax.fori_loop(first, end, lambda c, z: (fn(c), z)[1], 0)


def forward_pass(q, width, k_ref, vt_ref, e_ref, stat, acc, chunks, full, mask_of, scr):
    rows, qt, s_scr, m_scr, l_scr = scr
    cols = width * GROUP
    turned(q, width, rows, qt)
    tiles = tiles_of(cols, TILE)
    m_scr[:, :cols] = jnp.full((8, cols), -1e30, F32)
    l_scr[:, :cols] = jnp.zeros((8, cols), F32)
    acc[...] = jnp.zeros((HEAD, cols), F32)

    def score(c, masked):
        k = k_ref[at(c), :]
        for t in tiles:
            s = dot(k, qt[:, t])
            if masked:
                s = jnp.where(mask_of(c), s, -1e30)
            s_scr[at(c), t] = s
            m_scr[:, t] = jnp.maximum(m_scr[:, t], fold(s, jnp.max))

    loop(0, full, lambda c: score(c, False))
    loop(full, chunks, lambda c: score(c, True))
    top = jnp.max(m_scr[:, :cols], axis=0, keepdims=True) * (SCALE * LOG2E)
    m_scr[:, :cols] = jnp.broadcast_to(top, (8, cols))

    def weigh(c):
        for t in tiles:
            e = jnp.exp2(s_scr[at(c), t] * (SCALE * LOG2E) - m_scr[0:1, t])
            l_scr[:, t] += fold(e, jnp.sum)
            eb = e.astype(BF)
            e_ref[at(c), t] = eb
            acc[:, t] += dot(vt_ref[c], eb)

    loop(0, chunks, weigh)
    inv = 1.0 / jnp.sum(l_scr[:, :cols], axis=0, keepdims=True)
    acc[:, :cols] = acc[:, :cols] * inv
    stat[...] = jnp.broadcast_to(inv, (8, cols))


def backward_pass(q, g, width, v_ref, kt_ref, e_ref, stat, attn_t, dk_ref, dv_ref, chunks, scr):
    qs, gs, gt, acc, d_scr = scr
    cols = width * GROUP
    for h in range(GROUP):
        qs[h * width:(h + 1) * width, :] = q[:, h * HEAD:(h + 1) * HEAD]
    turned(g, width, gs, gt)
    for t in range(0, cols, HEAD):
        part = (gt[:, t:t + HEAD].astype(F32) * stat[0:1, t:t + HEAD]).astype(BF)
        gt[:, t:t + HEAD] = part
        gs[t:t + HEAD, :] = part.T
    tiles = tiles_of(cols, HALF)
    acc[:, :cols] = jnp.zeros((HEAD, cols), F32)
    delta = jnp.sum(attn_t[...] * gt[:, :cols].astype(F32), axis=0, keepdims=True)
    d_scr[:, :cols] = jnp.broadcast_to(delta, (8, cols))

    def back(c):
        v = v_ref[at(c), :]
        dk = dk_ref[at(c), :]
        dv = dv_ref[at(c), :]
        for t in tiles:
            e = e_ref[at(c), t]
            ds = (e.astype(F32) * (dot(v, gt[:, t]) - d_scr[0:1, t])).astype(BF)
            dv += dot(e, gs[t, :])
            dk += dot(ds, qs[t, :])
            acc[:, t] += dot(kt_ref[c], ds)
        dk_ref[at(c), :] = dk
        dv_ref[at(c), :] = dv

    loop(0, chunks, back)


def emit(src, width, scale, out, row, col):
    for t in range(width * GROUP // 128):
        x = (src[:, t * 128:(t + 1) * 128] * scale).T.astype(BF)
        per = 128 // width
        for i in range(per):
            h = t * per + i
            out[row:row + width, col + h * HEAD:col + (h + 1) * HEAD] = x[i * width:(i + 1) * width, :]


def chooser(sel):
    return (lax.broadcasted_iota(jnp.int32, (ROWS, ROWS), 0) == sel[0:1, :]).astype(F32)


def held_slots(sel, count):
    return jnp.where(lax.broadcasted_iota(jnp.int32, (1, ROWS), 1) < count[...], sel[...], -1)


def compact(sel):
    return chooser(sel).T[:SLOTS, :].astype(BF)


HALF = GROUP * HEAD
QG = 2 * HALF
KV = 2 * HEAD
DENSE = BLOCKS * ROWS
FEW = BLOCKS * SLOTS
SENT = ROWS + SLOTS
INVALID = 128.0
VMEM = pl.BlockSpec(memory_space=pltpu.VMEM)
SMEM = pl.BlockSpec(memory_space=pltpu.SMEM)
WHOLE = pltpu.CompilerParams(vmem_limit_bytes=60 << 20)
PARAMS = pltpu.CompilerParams(vmem_limit_bytes=16 << 20)
ANY = pl.BlockSpec(memory_space=pl.ANY)
SEL = pl.BlockSpec((1, ROWS), lambda i, info: (0, 0))


def own_head(shift):
    core, z = lax.rem(lax.axis_index("section"), 2), lax.div(lax.axis_index("ctx"), 4)
    return 2 * lax.rem(z + shift, 4) + core, core


def pack_kv_kernel(own, k_in, v_in, sel, sel_in, count, count_in, *outs):
    def mine(side, head):
        return own[:, pl.ds(pl.multiple_of(head * HEAD + side * HALF, HEAD), HEAD)]

    def theirs(side, head):
        return (k_in, v_in)[side][:, pl.ds(pl.multiple_of(head * HEAD, HEAD), HEAD)]

    def fill(dense, few, few_sel):
        pick = compact(few_sel)
        mark = INVALID * (1.0 - jnp.sum(pick.astype(F32), axis=1, keepdims=True))
        for step, out in enumerate(outs):
            for side in range(2):
                cols = slice(side * HEAD, (side + 1) * HEAD)
                out[:ROWS, cols] = dense(side, own_head(step)[0])
                rows = dot(pick, few(side, own_head(step)[0]))
                out[ROWS:, cols] = (rows if side else rows + mark).astype(BF)

    @pl.when(own_head(0)[1] == 1)
    def _():
        fill(mine, theirs, held_slots(sel_in, count_in))

    @pl.when(own_head(0)[1] == 0)
    def _():
        fill(theirs, mine, held_slots(sel, count))


def pack_kv(own, k_in, v_in, *slots):
    return list(pl.pallas_call(
        pack_kv_kernel,
        out_shape=[jax.ShapeDtypeStruct((SENT, KV), BF)] * 4,
        in_specs=[VMEM] * 7,
        out_specs=[VMEM] * 4,
        compiler_params=PARAMS,
        name="pack_kv",
    )(own, k_in, v_in, *slots))


def pack_kernel(own, come, sel, sel_in, count, count_in, o0, o1, o2, o3, held, sems):
    core = own_head(0)[1]
    outs, copies = (o0, o1, o2, o3), []
    for step in range(4):
        here = pl.ds(pl.multiple_of(own_head(step)[0] * HALF, HALF), HALF)
        for i, ref in enumerate((own, come)):
            copies.append(pltpu.make_async_copy(ref.at[:, here], held.at[step, i], sems.at[2 * step + i]))
            copies[-1].start()
    pick = compact(jnp.where(core == 1, held_slots(sel_in, count_in), held_slots(sel, count)))
    for step, out in enumerate(outs):
        copies[2 * step].wait()
        copies[2 * step + 1].wait()

        @pl.when(core == 1)
        def _(step=step, out=out):
            out[:ROWS, :] = held[step, 0]
            out[ROWS:, :] = dot(pick, held[step, 1]).astype(BF)

        @pl.when(core == 0)
        def _(step=step, out=out):
            out[:ROWS, :] = held[step, 1]
            out[ROWS:, :] = dot(pick, held[step, 0]).astype(BF)


def pack(own, come, slots, params):
    return list(pl.pallas_call(
        pack_kernel,
        out_shape=[jax.ShapeDtypeStruct((SENT, HALF), BF)] * 4,
        in_specs=[ANY] * 2 + [VMEM] * 4,
        out_specs=[VMEM] * 4,
        scratch_shapes=[pltpu.VMEM((4, 2, ROWS, HALF), BF), pltpu.SemaphoreType.DMA((8,))],
        compiler_params=params,
        name="pack",
    )(own, come, *slots))


FORTH = pltpu.CompilerParams(vmem_limit_bytes=12 << 20)
BACK = pltpu.CompilerParams(vmem_limit_bytes=24 << 20)
SUMS = [((DENSE, HEAD), F32)] * 2 + [((FEW, HEAD), F32)] * 2
FEWER = SLOTS * GROUP
LEFT = [((SENT, HALF), BF), ((DENSE, HALF), BF), ((8, HALF), F32), ((HEAD, HALF), F32),
        ((FEW, FEWER), BF), ((8, FEWER), F32), ((HEAD, FEWER), F32)]
KEYS = [((DENSE, HEAD), BF), ((DENSE // CHUNK, HEAD, CHUNK), BF), ((FEW, HEAD), BF), ((FEW // CHUNK, HEAD, CHUNK), BF)]
KEYED = KEYS + KEYS + [((FEW, HEAD), F32)]


def shaped(shapes):
    return [jax.ShapeDtypeStruct(s, d) for s, d in shapes]


def held(shapes):
    return [pltpu.VMEM(s, d) for s, d in shapes]


FORWARD = held([((HALF, HEAD), BF), ((HEAD, HALF), BF), ((DENSE, HALF), F32), ((8, HALF), F32), ((8, HALF), F32)])
BACKWARD = held([((HALF, HEAD), BF), ((HALF, HEAD), BF), ((HEAD, HALF), BF), ((HEAD, HALF), F32), ((8, HALF), F32)])


def cost(flops):
    return pl.CostEstimate(flops=int(flops), bytes_accessed=4 << 20, transcendentals=0)


def turn_blocks(x, xt):
    for c in range(xt.shape[0]):
        xt[c] = x[c * CHUNK:(c + 1) * CHUNK, :].T


def arrange(info, kvs, keyed):
    kd, ktd, kr, ktr, vd, vtd, vr, vtr, flags = keyed
    for ky, kv in enumerate(kvs):
        for kz in range(4):
            b = 4 * lax.rem(info[1] + 4 - kz, 4) + lax.rem(info[2] + 4 - ky, 4)
            big = pl.ds(pl.multiple_of(b * ROWS, ROWS), ROWS)
            small = pl.ds(pl.multiple_of(b * SLOTS, SLOTS), SLOTS)
            kd[big, :] = kv[kz, :ROWS, :HEAD]
            vd[big, :] = kv[kz, :ROWS, HEAD:]
            kr[small, :] = kv[kz, ROWS:, :HEAD]
            vr[small, :] = kv[kz, ROWS:, HEAD:]
            flags[small, :] = (kv[kz, ROWS:, :HEAD].astype(F32) < INVALID / 2).astype(F32)
    for x, xt in ((kd, ktd), (kr, ktr), (vd, vtd), (vr, vtr)):
        turn_blocks(x, xt)


def reach(info, shift):
    blk = 4 * lax.rem(info[1] + 4 - shift, 4) + info[2]
    per = CHUNK // ROWS
    return blk, lax.div(blk + per, per)


def forward_block(info, shift, q, keyed, left, scr):
    kd, _, kr, _, _, vtd, _, vtr, flags = keyed
    attn, e_dense, inv_dense, t_dense, e_few, inv_few, t_few = left
    blk, chunks = reach(info, shift)

    def place(cols):
        shape = (CHUNK, cols)
        return lax.broadcasted_iota(jnp.int32, shape, 0), lax.broadcasted_iota(jnp.int32, shape, 1)

    def causal(c):
        row, col = place(TILE)
        return c * CHUNK + row <= blk * ROWS + lax.rem(col, ROWS)

    def routed(c):
        row, col = place(FEWER)
        near = c * CHUNK + row <= blk * SLOTS + lax.rem(col, SLOTS)
        return near & (jnp.concatenate([flags[at(c), :]] * (FEWER // HEAD), axis=1) > 0.5)

    forward_pass(q[:ROWS, :], ROWS, kd, vtd, e_dense, inv_dense, t_dense, chunks, chunks - 1, causal, scr)
    emit(t_dense, ROWS, 1.0, attn, 0, 0)
    forward_pass(q[ROWS:, :], SLOTS, kr, vtr, e_few, inv_few, t_few, FEW // CHUNK, 0, routed, scr)
    emit(t_few, SLOTS, 1.0, attn, ROWS, 0)


def forward_kernel(shifts, first, info, *refs):
    n, m = len(shifts), len(LEFT)
    qs, refs = refs[:n], refs[n:]
    if first:
        kvs, refs = refs[:4], refs[4:]
    else:
        keyed, refs = refs[:9], refs[9:]
    lefts, refs = refs[:m * n], refs[m * n:]
    if first:
        keyed, refs = refs[:9], refs[9:]
        arrange(info, kvs, keyed)
    for i, shift in enumerate(shifts):
        forward_block(info, shift, qs[i], keyed, lefts[m * i:m * (i + 1)], refs)


def forward(shifts, info, qs, kvs=None, keyed=None):
    n, m, first = len(shifts), len(LEFT), kvs is not None
    shapes = LEFT * n + (KEYED if first else [])
    others = list(kvs if first else keyed)
    outs = pl.pallas_call(
        functools.partial(forward_kernel, shifts, first),
        out_shape=shaped(shapes),
        in_specs=[SMEM] + [VMEM] * (n + len(others)),
        out_specs=[VMEM] * len(shapes),
        scratch_shapes=FORWARD,
        compiler_params=FORTH,
        cost_estimate=cost(n * 4e9),
        name="forward",
    )(info, *qs, *others)
    lefts = [list(outs[m * i:m * (i + 1)]) for i in range(n)]
    return (lefts, outs[m * n:]) if first else lefts


def backward_block(info, shift, q, g, keyed, left, sums, dq, scr):
    _, ktd, _, ktr, vd, _, vr, _, _ = keyed
    _, chunks = reach(info, shift)
    backward_pass(q[:ROWS, :], g[:ROWS, :], ROWS, vd, ktd, *left[:3], *sums[:2], chunks, scr)
    emit(scr[3], ROWS, SCALE, dq, 0, 0)
    backward_pass(q[ROWS:, :], g[ROWS:, :], SLOTS, vr, ktr, *left[3:], *sums[2:], FEW // CHUNK, scr)
    emit(scr[3], SLOTS, SCALE, dq, ROWS, 0)


def backward_kernel(shifts, info, *refs):
    n, m = len(shifts), len(LEFT) - 1
    qs, gs, refs = refs[:n], refs[n:2 * n], refs[2 * n:]
    lefts, keyed, refs = refs[:m * n], refs[m * n:m * n + 9], refs[m * n + 9:]
    dqs, sent, sums, scr = refs[:n], refs[n:n + 4], refs[n + 4:n + 8], refs[n + 8:]
    for total in sums:
        total[...] = jnp.zeros_like(total)
    for i, shift in enumerate(shifts):
        backward_block(info, shift, qs[i], gs[i], keyed, lefts[m * i:m * (i + 1)], sums, dqs[i], scr)
    for ky in range(4):
        for kz in range(4):
            b = 4 * lax.rem(info[1] + kz, 4) + lax.rem(info[2] + ky, 4)
            big = pl.ds(pl.multiple_of(b * ROWS, ROWS), ROWS)
            small = pl.ds(pl.multiple_of(b * SLOTS, SLOTS), SLOTS)
            sent[ky][kz, :ROWS, :HEAD] = (sums[0][big, :] * SCALE).astype(BF)
            sent[ky][kz, :ROWS, HEAD:] = sums[1][big, :].astype(BF)
            sent[ky][kz, ROWS:, :HEAD] = (sums[2][small, :] * SCALE).astype(BF)
            sent[ky][kz, ROWS:, HEAD:] = sums[3][small, :].astype(BF)


def backward(shifts, info, qs, gs, lefts, keyed):
    n = len(shifts)
    shapes = [((SENT, HALF), BF)] * n + [((4, SENT, KV), BF)] * 4
    args = [qs[i] for i in shifts] + [gs[i] for i in shifts] + [x for i in shifts for x in lefts[i][1:]] + list(keyed)
    outs = pl.pallas_call(
        functools.partial(backward_kernel, shifts),
        out_shape=shaped(shapes),
        in_specs=[SMEM] + [VMEM] * len(args),
        out_specs=[VMEM] * len(shapes),
        scratch_shapes=held(SUMS) + BACKWARD,
        compiler_params=BACK,
        cost_estimate=cost(n * 6e9),
        name="backward",
    )(info, *args)
    return list(outs[:n]), list(outs[n:])


def fold_kernel(a, b, c, d, *outs):
    for i, out in enumerate(outs):
        total = a[i].astype(F32) + b[i].astype(F32) + c[i].astype(F32) + d[i].astype(F32)
        out[...] = total.astype(BF)


def fold_sums(parts):
    return list(pl.pallas_call(
        fold_kernel,
        out_shape=[jax.ShapeDtypeStruct((SENT, KV), BF)] * 4,
        in_specs=[VMEM] * 4,
        out_specs=[VMEM] * 4,
        compiler_params=PARAMS,
        name="fold_sums",
    )(*parts))


def heads_of(info, sel, mine, theirs, put):
    @pl.when(info[0] == 1)
    def _():
        put(0, theirs[0, :ROWS, :].astype(F32))
        put(1, mine[0, :ROWS, :].astype(F32))

    @pl.when(info[0] == 0)
    def _():
        pick = chooser(sel)[:, :SLOTS].astype(BF)
        put(0, dot(pick, mine[0, ROWS:, :]))
        put(1, dot(pick, theirs[0, ROWS:, :]))


def update_kernel(info, seg, mine, theirs, sel, out):
    def put(i, x):
        cols = slice(i * HALF, (i + 1) * HALF)
        out[:, cols] = (seg[:, cols].astype(F32) + x).astype(BF)

    heads_of(info, sel, mine, theirs, put)


def finish_q_kernel(info, mine, theirs, sel, out):
    def put(i, x):
        out[:, i * HALF:(i + 1) * HALF] = x.astype(BF)

    heads_of(info, sel, mine, theirs, put)


def by_head(kernel, name, info, seg, mine, theirs, sel):
    part = pl.BlockSpec((1, SENT, HALF), lambda i, info: (i, 0, 0))
    whole = pl.BlockSpec((ROWS, 2 * HALF), lambda i, info: (0, lax.rem(info[1] + i, 4)))
    segs = [] if seg is None else [seg]
    return pl.pallas_call(
        kernel,
        grid_spec=pltpu.PrefetchScalarGridSpec(
            num_scalar_prefetch=1,
            grid=(4,),
            in_specs=[whole] * len(segs) + [part, part, SEL],
            out_specs=whole,
        ),
        out_shape=jax.ShapeDtypeStruct((ROWS, 8 * HALF), BF),
        compiler_params=PARAMS,
        name=name,
    )(info, *segs, mine, theirs, sel)


def settle_kernel(x, out):
    out[...] = x[...]


def settle(x):
    part = pl.BlockSpec((ROWS, 2 * HALF), lambda i: (0, i))
    return pl.pallas_call(
        settle_kernel,
        grid=(4,),
        in_specs=[part],
        out_specs=part,
        out_shape=jax.ShapeDtypeStruct(x.shape, x.dtype),
        compiler_params=PARAMS,
        name="settle",
    )(x)


def finish_kv_kernel(info, sums, sums_in, sel, dk, dv):
    def fill(even, odd, rows):
        for shift in range(4):
            for i, ref in enumerate((even, odd)):
                head = 2 * lax.rem(info[1] + 4 - shift, 4) + i
                at = pl.ds(pl.multiple_of(head * HEAD, HEAD), HEAD)
                x = rows(ref[shift])
                dk[:, at] = x[:, :HEAD]
                dv[:, at] = x[:, HEAD:]

    @pl.when(info[0] == 1)
    def _():
        fill(sums_in, sums, lambda x: x[:ROWS, :])

    @pl.when(info[0] == 0)
    def _():
        pick = chooser(sel)[:, :SLOTS].astype(BF)
        fill(sums, sums_in, lambda x: dot(pick, x[ROWS:, :]).astype(BF))


def finish_kv(info, sums, sums_in, sel):
    return pl.pallas_call(
        finish_kv_kernel,
        out_shape=[jax.ShapeDtypeStruct((ROWS, 8 * HEAD), BF)] * 2,
        in_specs=[SMEM] + [VMEM] * 3,
        out_specs=[VMEM] * 2,
        compiler_params=PARAMS,
        name="finish_kv",
    )(info, sums, sums_in, sel)


def along_z(x, by):
    return lax.ppermute(x, "ctx", [(4 * z + y, 4 * ((z + by) % 4) + y) for z in range(4) for y in range(4)])


def along_y(x, by):
    return lax.ppermute(x, "ctx", [(4 * z + y, 4 * z + (y + by) % 4) for z in range(4) for y in range(4)])


def swap(x):
    return lax.ppermute(x, "section", [(i, i ^ 1) for i in range(8)])


def onward(x):
    return lax.ppermute(x, "section", [(i, i + 1) for i in range(7)])


def both(*xs):
    return lax.optimization_barrier(xs)


def body(segment_input, queries, keys, values, cotangent, selected, counts):
    section, place = lax.axis_index("section"), lax.axis_index("ctx")
    info = jnp.stack([section % 2, place // 4, place % 4]).astype(jnp.int32)
    seg, q, k, v, g = (x[0] for x in (segment_input, queries, keys, values, cotangent))
    sel = jnp.where(jnp.arange(ROWS, dtype=jnp.int32)[None, :] < counts, selected, -1)

    own = jnp.concatenate([k, v], 1)
    k_in, v_in = swap(k), swap(v)
    slots = selected, swap(selected), counts, swap(counts)
    kv = pack_kv(own, k_in, v_in, *slots)
    q, g, *_ = both(q, g, k_in, v_in, slots[1], slots[3])
    q_in, g_in = swap(q), swap(g)
    qs = pack(q, q_in, slots, WHOLE)
    for by in (1, 3, 2):
        kv[by] = along_z(kv[by], by)
    kv[1], kv[2], kv[3], qs[1], qs[2], qs[3], g_in = both(kv[1], kv[2], kv[3], qs[1], qs[2], qs[3], g_in)
    column = jnp.stack(kv)
    kvs = [column] + [along_y(column, by) for by in (1, 2, 3)]
    qs[1], qs[2], qs[3], g_in, _ = both(qs[1], qs[2], qs[3], g_in, column)
    for by in (1, 3, 2):
        qs[by] = along_z(qs[by], by)
    gs = pack(g, g_in, slots, PARAMS)

    qs[0], qs[1], qs[3] = both(qs[0], qs[1], qs[3])
    (own,), keyed = forward((0,), info, [qs[0]], kvs=kvs)
    for by in (1, 3, 2):
        gs[by] = along_z(gs[by], by)
    one, three, two = forward((1, 3, 2), info, [qs[1], qs[3], qs[2]], keyed=keyed)
    lefts = [own, one, two, three]
    attn = [along_z(lefts[by][0], 4 - by) if by else lefts[by][0] for by in range(4)]
    dq, sent = backward((1, 3, 0, 2), info, qs, gs, lefts, keyed)
    dq = [dq[2], dq[0], dq[3], dq[1]]
    dq = [along_z(dq[by], 4 - by) if by else dq[by] for by in range(4)]
    attn[1], attn[2], attn[3], sent[0] = both(attn[1], attn[2], attn[3], sent[0])
    dq[1], dq[3], sent[1] = both(dq[1], dq[3], sent[1])
    attn = jnp.stack(attn)
    updated = by_head(update_kernel, "update", info, seg, attn, swap(attn), sel)
    next_input = onward(updated)
    sums = fold_sums([sent[0]] + [along_y(sent[by], by) for by in (1, 2, 3)])
    dq[2], sums[0] = both(dq[2], sums[0])
    dq = jnp.stack(dq)
    query_grad = by_head(finish_q_kernel, "finish_q", info, None, dq, swap(dq), sel)
    sums = [sums[0]] + [along_z(sums[by], by) for by in (1, 2, 3)]
    next_input, query_grad, *sums = both(settle(next_input), query_grad, *sums)
    sums = jnp.stack(sums)
    key_grad, value_grad = finish_kv(info, sums, swap(sums), sel)
    return next_input[None], query_grad[None], key_grad[None], value_grad[None]


def solution(mesh):
    wide, thin = P("section", "ctx", None), P("section", "ctx")
    return jax.shard_map(
        body,
        mesh=mesh,
        in_specs=(wide,) * 5 + (thin,) * 2,
        out_specs=(wide,) * 4,
        check_vma=False,
    )
```
